32 devices in a mesh: grp: 4 (over y, x), shard: 8 (over z, core).
Axes of the slice: x: 2, y: 2, z: 4, core: 2. Of those that a mesh axis runs over, the one named last changes fastest.
Arguments:
- token_table: bfloat16 [30720, 768], P('shard'), may hold values from -6 to 6
- enc_weight: bfloat16 [768, 768], replicated, may hold values from -0.21875 to 0.21875
- enc_gain: float32 [768], replicated, may hold values from 0.1 to 1.9
- label_tokens: int32 [4096, 8], P(('grp', 'shard')), may hold values from 0 to 30719, as said below
- ref_owner: int32 [4096, 1], P(('grp', 'shard')), may hold values from 0 to 7; in each aligned block of 128 rows (0 to 127, 128 to 255, ...) at most 32 rows name the same one
- ref_row: int32 [4096], P(('grp', 'shard')), may hold values from 0 to 1279
- free_rows: bfloat16 [40960, 768], P(('grp', 'shard')), may hold values from -0.21875 to 0.21875
- docs: bfloat16 [64, 768], P(('grp', 'shard')), may hold values from -6 to 6
- positives: int32 [64, 5], P(('grp', 'shard')), may hold values from 0 to 40959
Outputs:
- free_grad: bfloat16 [40960, 768], P(('grp', 'shard'))
- doc_grad: float32 [64, 768], P(('grp', 'shard'))
- ref_grad: bfloat16 [4096, 768], P(('grp', 'shard'))
The draws below stay inside these ranges and needn't reach their ends.
Inputs may be any that keep to these rules, and one draw needn't show every extreme that they name: `label_tokens`: among the 1024 tokens of one device's labels, at most 160 lie in any one block of 3840 consecutive ids, and some block holds exactly 160 of them. `ref_owner`: among one device's 128 refreshed labels at most 32 name one owner.
All inputs are finite; a program needn't handle non-finite values.
Results may differ from the reference program's by a relative error of at most 0.0055.
Values may be sent and summed in bfloat16 or wider, within the bound.
No kernel may reach another device: no remote copies, remote signals or barrier semaphores. Data moves between devices by JAX's collectives and lax.ppermute only.
A program may use at most 64 MiB of HBM per device.

```python
import math
import jax
import jax.numpy as jnp
import numpy as np
from jax import lax

D = 768
VOCAB = 30720
LAB_DEV = 1280
POS = 5
LEN = 8
REF_DEV = 128
DOCS = 64
SLAB = 40960
REFS = 4096
CAP = 32
TCAP = 160
N_GRP = 4
N_SHARD = 8


def draw_label_tokens(key, part):
    key = jax.random.fold_in(key, 11)
    token_count = REF_DEV * LEN
    vocab_rows = VOCAB // N_SHARD

    def one_block(block_key):
        first_key, order_key, mix_key, local_key = jax.random.split(block_key, 4)
        owners = jnp.repeat(jnp.arange(N_SHARD, dtype=jnp.int32), TCAP)
        chosen_owner = jax.random.randint(first_key, (), 0, N_SHARD, dtype=jnp.int32)
        ranking = jax.random.permutation(order_key, owners.shape[0]).astype(jnp.int32)
        scores = jnp.where(owners == chosen_owner, 0, 1).astype(jnp.int32) * owners.shape[0] + ranking
        picked = owners[jnp.argsort(scores)[:token_count]]
        picked = picked[jax.random.permutation(mix_key, token_count)]
        offsets = jax.random.randint(local_key, (token_count,), 0, vocab_rows, dtype=jnp.int32)
        return picked * vocab_rows + offsets
    keys = jax.random.split(key, REFS // REF_DEV)
    return jax.vmap(one_block)(keys).reshape(REFS, LEN).astype(jnp.int32)


def with_ends(result, key, low, high):
    spot = [jax.random.randint(jax.random.fold_in(key, axis), (), 0, length) for axis, length in enumerate(result.shape)]
    widest = result.shape.index(max(result.shape))
    neighbour = spot[:widest] + [(spot[widest] + 1) % result.shape[widest]] + spot[widest + 1:]
    return result.at[tuple(spot)].set(low).at[tuple(neighbour)].set(high)


def level_of(own_key, shape, cuts, smallest, largest):
    factor_of, own = 1.0, jax.random.fold_in(own_key, 6)
    for dim, shards_of in cuts:
        draws = jnp.exp(jax.random.uniform(jax.random.fold_in(own, dim), (shards_of,), jnp.float32, smallest / len(cuts), largest / len(cuts)))
        factor_of = factor_of * jnp.repeat(draws, shape[dim] // shards_of).reshape([-1 if axis == dim else 1 for axis in range(len(shape))])
    return factor_of


def assign_block(key, own, number, rows, number_of, top, limit, skew):
    sequence = jax.random.permutation(key, number_of)
    packed, usual = load_shares(number_of, rows * top, limit, skew, True), load_shares(number_of, rows * top, limit, skew, False)
    places = jnp.arange(number_of)

    def named(sizes, offset_by):
        used = int((sizes > 0).sum())
        fixed = max(1, used // 4)
        shifted = fixed + (places - fixed + offset_by * (used - fixed)) % max(1, number_of - fixed)
        return jnp.zeros((number_of,), jnp.int32).at[sequence[jnp.where(places < fixed, places, shifted)]].set(jnp.asarray(sizes, jnp.int32))

    sizes = jnp.where(number % 4 == 0, named(packed, number // 4), named(usual, number - number // 4 - 1))
    mixed = jax.random.permutation(jax.random.fold_in(own, 3), number_of)
    source_of, sink = mixed[0:number_of // 2 * 2:2], mixed[1:number_of // 2 * 2:2]
    slack = jnp.minimum(sizes[source_of] - 1, limit - sizes[sink]) // 2
    slack = jnp.where((source_of == sequence[0]) | (sink == sequence[0]) | (sizes[sink] == 0), 0, jnp.maximum(slack, 0))
    shifted = jax.random.randint(jax.random.fold_in(own, 4), (number_of // 2,), 0, 1 << 20) % (slack + 1)
    sizes = sizes.at[source_of].add(-shifted).at[sink].add(shifted)
    items = jnp.searchsorted(jnp.cumsum(sizes), jnp.arange(rows * top), side="right").astype(jnp.int32)
    grid = items.reshape(top, rows).T
    grid = grid[jax.random.permutation(jax.random.fold_in(own, 1), rows)]
    offset_by = jax.random.randint(jax.random.fold_in(own, 2), (rows, 1), 0, top)
    return jnp.take_along_axis(grid, (jnp.arange(top)[None, :] + offset_by) % top, axis=1)


def load_shares(number_of, total, most, slope, full):
    loads = [(1 << 20) // math.isqrt(grade ** slope) + 1 for grade in range(1, number_of + 1)]
    largest = most if full else min(most, max(-(-total // number_of), total * loads[0] // sum(loads)))
    least = 1 if total - largest >= number_of - 1 else 0
    given, surplus = [largest] + [least] * (number_of - 1), total - largest - least * (number_of - 1)
    while surplus > 0:
        free = [i for i in range(1, number_of) if given[i] < largest] or [i for i in range(1, number_of) if given[i] < most]
        pool, left = sum([loads[i] for i in free]), surplus
        for i in free:
            extra = min(most - given[i], max(1, left * loads[i] // pool), surplus)
            given[i] = given[i] + extra
            surplus = surplus - extra
    return np.array(given)


def noise(rng, dims, deviation, reach, shards=(), kind=jnp.bfloat16):
    loudness = level_of(rng, dims, shards, -0.22, 0.18) if shards else 1.0
    array = jax.random.normal(rng, dims, jnp.float32) * deviation * loudness
    return jnp.minimum(jnp.maximum(array, -reach), reach).astype(kind)


def setup_inputs(seed: int = 0) -> dict:
    arg_keys = jax.random.split(jax.random.key(seed), 10)
    token_table = noise(arg_keys[0], (VOCAB, D), 1.0, 6.0, ((0, 8),))
    enc_weight = noise(arg_keys[1], (D, D), D ** -0.5, 0.21875)
    enc_gain = jnp.clip(1.0 + 0.18 * jax.random.normal(arg_keys[2], (D,), jnp.float32), 0.1, 1.9)
    label_tokens = draw_label_tokens(jax.random.fold_in(arg_keys[9], 71), 0)
    ref_owner_keys = jax.random.split(jax.random.fold_in(arg_keys[4], 1), REFS // REF_DEV)
    ref_owner_turns = jax.random.permutation(jax.random.fold_in(arg_keys[4], 3), REFS // REF_DEV)
    ref_owner = jax.vmap(lambda own, number: assign_block(jax.random.fold_in(arg_keys[4], 2), own, number, REF_DEV, N_SHARD, 1, CAP, 2))(ref_owner_keys, ref_owner_turns).reshape((REFS, 1))
    ref_row = with_ends(jax.random.randint(arg_keys[5], (REFS,), 0, LAB_DEV), jax.random.fold_in(arg_keys[5], 1), 0, LAB_DEV - 1).astype(jnp.int32)
    free_rows = noise(arg_keys[6], (SLAB, D), D ** -0.5, 0.21875, ((0, 32),))
    docs = noise(arg_keys[7], (DOCS, D), 1.0, 6.0, ((0, 32),))
    positives = with_ends(jax.random.randint(arg_keys[8], (DOCS, POS), 0, SLAB), jax.random.fold_in(arg_keys[8], 1), 0, SLAB - 1).astype(jnp.int32)
    return {"token_table": token_table, "enc_weight": enc_weight, "enc_gain": enc_gain, "label_tokens": label_tokens, "ref_owner": ref_owner, "ref_row": ref_row, "free_rows": free_rows, "docs": docs, "positives": positives}


def encode_block(token_table, enc_weight, enc_gain, block):
    embedded = token_table[block].astype(jnp.float32)
    pooled = lax.optimization_barrier(jnp.mean(embedded, axis=1)).astype(jnp.bfloat16)
    projected = jnp.dot(pooled, enc_weight, preferred_element_type=jnp.float32)
    scale = lax.rsqrt(lax.optimization_barrier(jnp.mean(projected * projected, axis=1, keepdims=True)) + 1e-06)
    return (projected * scale * enc_gain * D ** (-0.5)).astype(jnp.bfloat16)

def reference(token_table, enc_weight, enc_gain, label_tokens, ref_owner, ref_row, free_rows, docs, positives):
    blocks = label_tokens.reshape(REFS // REF_DEV, REF_DEV, LEN)
    encoded = lax.map(lambda block: encode_block(token_table, enc_weight, enc_gain, block), blocks).reshape(REFS, D)
    group = jnp.arange(REFS, dtype=jnp.int32) // (REF_DEV * N_SHARD)
    slab_id = ((group * N_SHARD + ref_owner[:, 0]) * LAB_DEV + ref_row).astype(jnp.int32)
    local_cols = jnp.arange(LAB_DEV, dtype=jnp.int32)

    def one_shard(doc_total, shard):
        base = shard * LAB_DEV
        local = slab_id - base
        inside = (local >= 0) & (local < LAB_DEV)
        target = jnp.where(inside, local, LAB_DEV)
        delta = jnp.zeros((LAB_DEV, D), jnp.float32).at[target].add(encoded.astype(jnp.float32), mode='drop')
        free_part = lax.dynamic_slice_in_dim(free_rows, base, LAB_DEV, 0)
        head = (free_part.astype(jnp.float32) + delta).astype(jnp.bfloat16)
        logits = lax.dot_general(docs, head, (((1,), (1,)), ((), ())), preferred_element_type=jnp.float32)
        hits = jnp.zeros(logits.shape, jnp.bool_)
        for column in range(POS):
            hits = hits | (positives[:, column:column + 1] == (base + local_cols)[None, :])
        errors = (jax.nn.sigmoid(logits) - hits.astype(jnp.float32)).astype(jnp.bfloat16)
        grad_part = lax.dot_general(errors, docs, (((0,), (0,)), ((), ())), preferred_element_type=jnp.float32)
        doc_total = doc_total + jnp.dot(errors, head, preferred_element_type=jnp.float32)
        return (doc_total, grad_part.astype(jnp.bfloat16))
    doc_grad, grads = lax.scan(one_shard, jnp.zeros((DOCS, D), jnp.float32), jnp.arange(N_GRP * N_SHARD, dtype=jnp.int32))
    free_grad = grads.reshape(SLAB, D)
    ref_grad = free_grad[slab_id]
    return (free_grad, doc_grad, ref_grad)
```

```python
import jax
import jax.numpy as jnp
from jax import lax
from jax.sharding import PartitionSpec as P

BF16 = jnp.bfloat16
F32 = jnp.float32
I32 = jnp.int32
ALL = ("grp", "shard")


def exchange(blocks, axes):
    return lax.all_to_all(blocks, axes, split_axis=0, concat_axis=0, tiled=True)


def inclusive_counts(marks):
    count = marks.shape[0]
    rows = lax.broadcasted_iota(I32, (count, count), 0)
    cols = lax.broadcasted_iota(I32, (count, count), 1)
    return jnp.dot((cols <= rows).astype(BF16), marks.astype(BF16), preferred_element_type=F32).astype(I32)


def token_places(owner, shards, cap):
    labels, length = owner.shape
    marks = (owner[:, :, None] == jnp.arange(shards, dtype=I32)).astype(I32)
    within = inclusive_counts(marks.reshape(labels, length * shards)).reshape(labels, length, shards)
    totals = within[-1]
    before = jnp.cumsum(totals, axis=0) - totals
    slot = jnp.sum((within + before[None] - 1) * marks, axis=2)
    return owner * cap + slot


def label_places(owner, shards, cap):
    marks = (owner[:, None] == jnp.arange(shards, dtype=I32)).astype(I32)
    slot = jnp.sum((inclusive_counts(marks) - 1) * marks, axis=1)
    return owner * cap + slot


def placed(values, places, size):
    hit = places[:, None] == jnp.arange(size, dtype=I32)[None, :]
    return jnp.sum(jnp.where(hit, values[:, None] + 1, 0), axis=0) - 1


def on_device(
    token_table, enc_weight, enc_gain, label_tokens, ref_owner, ref_row, free_rows, docs, positives
):
    shards = lax.axis_size("shard")
    devices = shards * lax.axis_size("grp")
    vocab_rows, width = token_table.shape
    labels, length = label_tokens.shape
    own_docs = docs.shape[0]
    pos_count = positives.shape[1]
    slab_rows = free_rows.shape[0]
    tokens = labels * length
    token_cap = 5 * tokens // (4 * shards)
    label_cap = 2 * labels // shards

    token_owner = label_tokens // vocab_rows
    token_dest = token_places(token_owner, shards, token_cap)
    send_ids = placed(
        (label_tokens - token_owner * vocab_rows).reshape(tokens),
        token_dest.reshape(tokens),
        shards * token_cap,
    )
    label_dest = label_places(ref_owner[:, 0], shards, label_cap)
    send_rows = placed(ref_row, label_dest, shards * label_cap)
    asked = exchange(
        jnp.concatenate(
            [send_ids.reshape(shards, token_cap), send_rows.reshape(shards, label_cap)], axis=1
        ),
        "shard",
    )
    got_rows = asked[:, token_cap:].reshape(shards * label_cap)

    digits = jnp.concatenate(
        [positives & 255, (positives >> 8) & 255, positives >> 16], axis=1
    ).astype(BF16)
    own_block = jnp.concatenate(
        [docs, digits, jnp.zeros((own_docs, 128 - 3 * pos_count), BF16)], axis=1
    )
    all_blocks = exchange(
        jnp.broadcast_to(own_block[None], (devices, own_docs, width + 128)), ALL
    ).reshape(devices * own_docs, width + 128)
    all_docs = all_blocks[:, :width]
    d = all_blocks[:, width : width + 3 * pos_count].astype(I32)
    all_positives = d[:, :pos_count] + 256 * d[:, pos_count : 2 * pos_count] + 65536 * d[:, 2 * pos_count :]

    found = token_table[jnp.maximum(asked[:, :token_cap], 0)]
    token_found = exchange(found, "shard").reshape(shards * token_cap, width)
    pick_tokens = jnp.zeros((labels, shards * token_cap), F32)
    for j in range(length):
        pick_tokens += (
            token_dest[:, j : j + 1] == jnp.arange(shards * token_cap, dtype=I32)[None, :]
        ).astype(F32)
    pooled = jnp.dot(
        (pick_tokens / length).astype(BF16), token_found, preferred_element_type=F32
    ).astype(BF16)
    projected = jnp.dot(pooled, enc_weight, preferred_element_type=F32)
    norm_scale = lax.rsqrt(jnp.mean(projected * projected, axis=1, keepdims=True) + 1e-06)
    encoded = (projected * norm_scale * enc_gain * width ** (-0.5)).astype(BF16)

    to_slots = (
        jnp.arange(shards * label_cap, dtype=I32)[:, None] == label_dest[None, :]
    ).astype(BF16)
    send_vectors = jnp.dot(to_slots, encoded, preferred_element_type=F32).astype(BF16)
    got_vectors = exchange(send_vectors.reshape(shards, label_cap, width), "shard").reshape(
        shards * label_cap, width
    )
    to_rows = (jnp.arange(slab_rows, dtype=I32)[:, None] == got_rows[None, :]).astype(BF16)
    delta = jnp.dot(to_rows, got_vectors, preferred_element_type=F32)
    head = (free_rows.astype(F32) + delta).astype(BF16)

    label_columns = lax.axis_index(ALL) * slab_rows + jnp.arange(slab_rows, dtype=I32)
    logits = lax.dot_general(all_docs, head, (((1,), (1,)), ((), ())), preferred_element_type=F32)
    hits = jnp.zeros(logits.shape, jnp.bool_)
    for column in range(pos_count):
        hits = hits | (all_positives[:, column : column + 1] == label_columns[None, :])
    errors = (jax.nn.sigmoid(logits) - hits.astype(F32)).astype(BF16)
    doc_terms = jnp.dot(errors, head, preferred_element_type=F32)
    free_grad = lax.dot_general(
        errors, all_docs, (((0,), (0,)), ((), ())), preferred_element_type=F32
    ).astype(BF16)
    picked = lax.dot_general(
        to_rows, errors, (((0,), (1,)), ((), ())), preferred_element_type=F32
    ).astype(BF16)
    returned = exchange(picked.reshape(shards, label_cap, devices * own_docs), "shard").reshape(
        shards * label_cap, devices * own_docs
    )
    ref_errors = lax.dot_general(
        to_slots, returned, (((0,), (0,)), ((), ())), preferred_element_type=F32
    ).astype(BF16)
    ref_grad = jnp.dot(ref_errors, all_docs, preferred_element_type=F32).astype(BF16)
    doc_grad = jnp.sum(exchange(doc_terms.reshape(devices, own_docs, width), ALL), axis=0)
    return (free_grad, doc_grad, ref_grad)


def solution(mesh):
    in_specs = (
        P("shard", None),
        P(),
        P(),
        P(ALL, None),
        P(ALL, None),
        P(ALL),
        P(ALL, None),
        P(ALL, None),
        P(ALL, None),
    )
    out_specs = (P(ALL, None), P(ALL, None), P(ALL, None))
    return jax.shard_map(
        on_device, mesh=mesh, in_specs=in_specs, out_specs=out_specs, check_vma=False
    )
```

```python
import jax
import jax.numpy as jnp
from jax import lax
from jax.sharding import PartitionSpec as P

BF16 = jnp.bfloat16
F32 = jnp.float32
I32 = jnp.int32
ALL = ("grp", "shard")


def exchange(blocks, axes):
    return lax.all_to_all(blocks, axes, split_axis=0, concat_axis=0, tiled=True)


def inclusive_counts(marks):
    count = marks.shape[0]
    rows = lax.broadcasted_iota(I32, (count, count), 0)
    cols = lax.broadcasted_iota(I32, (count, count), 1)
    return jnp.dot((cols <= rows).astype(BF16), marks.astype(BF16), preferred_element_type=F32).astype(I32)


def token_places(owner, shards, cap):
    labels, length = owner.shape
    marks = (owner[:, :, None] == jnp.arange(shards, dtype=I32)).astype(I32)
    within = inclusive_counts(marks.reshape(labels, length * shards)).reshape(labels, length, shards)
    totals = within[-1]
    before = jnp.cumsum(totals, axis=0) - totals
    slot = jnp.sum((within + before[None] - 1) * marks, axis=2)
    return owner * cap + slot


def label_places(owner, shards, cap):
    marks = (owner[:, None] == jnp.arange(shards, dtype=I32)).astype(I32)
    slot = jnp.sum((inclusive_counts(marks) - 1) * marks, axis=1)
    return owner * cap + slot


def placed(values, places, size):
    hit = places[:, None] == jnp.arange(size, dtype=I32)[None, :]
    return jnp.sum(jnp.where(hit, values[:, None] + 1, 0), axis=0) - 1


def swap_cores(x):
    return lax.ppermute(x, "shard", [(i, i ^ 1) for i in range(lax.axis_size("shard"))])


def to_chip(x, k):
    return lax.ppermute(x, "shard", [(i, i ^ (2 * k)) for i in range(lax.axis_size("shard"))])


def by_rows(
    token_table, enc_weight, enc_gain, label_tokens, ref_owner, ref_row, free_rows, docs, positives
):
    shards = lax.axis_size("shard")
    devices = shards * lax.axis_size("grp")
    vocab_rows, width = token_table.shape
    labels, length = label_tokens.shape
    own_docs = docs.shape[0]
    pos_count = positives.shape[1]
    slab_rows = free_rows.shape[0]
    tokens = labels * length
    token_cap = 5 * tokens // (4 * shards)
    label_cap = 2 * labels // shards

    token_owner = label_tokens // vocab_rows
    token_dest = token_places(token_owner, shards, token_cap)
    send_ids = placed(
        (label_tokens - token_owner * vocab_rows).reshape(tokens),
        token_dest.reshape(tokens),
        shards * token_cap,
    )
    label_dest = label_places(ref_owner[:, 0], shards, label_cap)
    send_rows = placed(ref_row, label_dest, shards * label_cap)
    asked = exchange(
        jnp.concatenate(
            [send_ids.reshape(shards, token_cap), send_rows.reshape(shards, label_cap)], axis=1
        ),
        "shard",
    )
    got_rows = asked[:, token_cap:].reshape(shards * label_cap)

    digits = jnp.concatenate(
        [positives & 255, (positives >> 8) & 255, positives >> 16], axis=1
    ).astype(BF16)
    own_block = jnp.concatenate(
        [docs, digits, jnp.zeros((own_docs, 128 - 3 * pos_count), BF16)], axis=1
    )
    all_blocks = exchange(
        jnp.broadcast_to(own_block[None], (devices, own_docs, width + 128)), ALL
    ).reshape(devices * own_docs, width + 128)
    all_docs = all_blocks[:, :width]
    d = all_blocks[:, width : width + 3 * pos_count].astype(I32)
    all_positives = d[:, :pos_count] + 256 * d[:, pos_count : 2 * pos_count] + 65536 * d[:, 2 * pos_count :]

    found = token_table[jnp.maximum(asked[:, :token_cap], 0)]
    token_found = exchange(found, "shard").reshape(shards * token_cap, width)
    pick_tokens = jnp.zeros((labels, shards * token_cap), F32)
    for j in range(length):
        pick_tokens += (
            token_dest[:, j : j + 1] == jnp.arange(shards * token_cap, dtype=I32)[None, :]
        ).astype(F32)
    pooled = jnp.dot(
        (pick_tokens / length).astype(BF16), token_found, preferred_element_type=F32
    ).astype(BF16)
    projected = jnp.dot(pooled, enc_weight, preferred_element_type=F32)
    norm_scale = lax.rsqrt(jnp.mean(projected * projected, axis=1, keepdims=True) + 1e-06)
    encoded = (projected * norm_scale * enc_gain * width ** (-0.5)).astype(BF16)

    to_slots = (
        jnp.arange(shards * label_cap, dtype=I32)[:, None] == label_dest[None, :]
    ).astype(BF16)
    send_vectors = jnp.dot(to_slots, encoded, preferred_element_type=F32).astype(BF16)
    got_vectors = exchange(send_vectors.reshape(shards, label_cap, width), "shard").reshape(
        shards * label_cap, width
    )
    to_rows = (jnp.arange(slab_rows, dtype=I32)[:, None] == got_rows[None, :]).astype(BF16)
    delta = jnp.dot(to_rows, got_vectors, preferred_element_type=F32)
    head = (free_rows.astype(F32) + delta).astype(BF16)

    label_columns = lax.axis_index(ALL) * slab_rows + jnp.arange(slab_rows, dtype=I32)
    logits = lax.dot_general(all_docs, head, (((1,), (1,)), ((), ())), preferred_element_type=F32)
    hits = jnp.zeros(logits.shape, jnp.bool_)
    for column in range(pos_count):
        hits = hits | (all_positives[:, column : column + 1] == label_columns[None, :])
    errors = (jax.nn.sigmoid(logits) - hits.astype(F32)).astype(BF16)
    doc_terms = jnp.dot(errors, head, preferred_element_type=F32)
    free_grad = lax.dot_general(
        errors, all_docs, (((0,), (0,)), ((), ())), preferred_element_type=F32
    ).astype(BF16)
    picked = lax.dot_general(
        to_rows, errors, (((0,), (1,)), ((), ())), preferred_element_type=F32
    ).astype(BF16)
    returned = exchange(picked.reshape(shards, label_cap, devices * own_docs), "shard").reshape(
        shards * label_cap, devices * own_docs
    )
    ref_errors = lax.dot_general(
        to_slots, returned, (((0,), (0,)), ((), ())), preferred_element_type=F32
    ).astype(BF16)
    ref_grad = jnp.dot(ref_errors, all_docs, preferred_element_type=F32).astype(BF16)
    doc_grad = jnp.sum(exchange(doc_terms.reshape(devices, own_docs, width), ALL), axis=0)
    return (free_grad, doc_grad, ref_grad)


def by_sums(
    token_table, enc_weight, enc_gain, label_tokens, ref_owner, ref_row, free_rows, docs, positives
):
    shards = lax.axis_size("shard")
    chips = shards // 2
    devices = shards * lax.axis_size("grp")
    me = lax.axis_index("shard")
    vocab_rows, width = token_table.shape
    labels, length = label_tokens.shape
    own_docs = docs.shape[0]
    all_count = devices * own_docs
    pos_count = positives.shape[1]
    slab_rows = free_rows.shape[0]
    tokens = labels * length
    token_cap = 5 * tokens // (4 * shards)
    label_cap = 2 * labels // shards
    others = [k for k in range(chips - 1, 0, -1)]
    stride = 2 * labels

    other_table = swap_cores(token_table)

    token_owner = label_tokens // vocab_rows
    token_dest = token_places(token_owner ^ me, shards, token_cap)
    codes = (label_tokens - token_owner * vocab_rows) * stride + jnp.arange(labels, dtype=I32)[:, None]
    hit = token_dest.reshape(tokens)[:, None] == jnp.arange(shards * token_cap, dtype=I32)[None, :]
    asks = labels + jnp.sum(jnp.where(hit, codes.reshape(tokens)[:, None] - labels, 0), axis=0)
    asks = asks.reshape(chips, 2 * token_cap)
    asked = {k: to_chip(asks[k : k + 1], k) for k in others}
    asked[0] = asks[0:1]

    label_dest = label_places(ref_owner[:, 0] ^ me, shards, label_cap)
    mine = jnp.stack([label_dest, ref_row])
    theirs = swap_cores(mine)
    own_rel = label_dest // label_cap
    other_rel = theirs[0] // label_cap
    places = jnp.concatenate(
        [
            jnp.where(own_rel % 2 == 0, label_dest, -1),
            jnp.where(other_rel % 2 == 1, theirs[0], -1),
        ]
    )
    slots = shards * label_cap
    to_slots = jnp.arange(slots, dtype=I32)[:, None] == places[None, :]
    chip_rows = jnp.concatenate([ref_row, theirs[1]])
    send_rows = jnp.sum(jnp.where(to_slots, chip_rows[None, :] + 1, 0), axis=1) - 1
    send_rows = send_rows.reshape(chips, 2 * label_cap)
    to_slots = to_slots.astype(BF16)
    got_rows = jnp.concatenate(
        [send_rows[0:1]] + [to_chip(send_rows[k : k + 1], k) for k in range(1, chips)]
    ).reshape(slots)

    digits = jnp.concatenate(
        [positives & 255, (positives >> 8) & 255, positives >> 16], axis=1
    ).astype(BF16)
    own_block = jnp.concatenate(
        [docs, digits, jnp.zeros((own_docs, 128 - 3 * pos_count), BF16)], axis=1
    )
    all_blocks = exchange(
        jnp.broadcast_to(own_block[None], (devices, own_docs, width + 128)), ALL
    ).reshape(all_count, width + 128)
    all_docs = all_blocks[:, :width]
    d = all_blocks[:, width : width + 3 * pos_count].astype(I32)
    all_positives = d[:, :pos_count] + 256 * d[:, pos_count : 2 * pos_count] + 65536 * d[:, 2 * pos_count :]

    def partial(code):
        ids = code[0] // stride
        which = code[0] - ids * stride
        pick = (jnp.arange(labels, dtype=I32)[:, None] == which[None, :]).astype(BF16) / length
        near = token_table[ids[:token_cap]]
        far = other_table[ids[token_cap:]]
        return jnp.dot(pick[:, :token_cap], near, preferred_element_type=F32) + jnp.dot(
            pick[:, token_cap:], far, preferred_element_type=F32
        )

    arrived = [to_chip(partial(asked[k]).astype(BF16), k) for k in others]
    pooled = partial(asked[0])
    for term in arrived:
        pooled = pooled + term.astype(F32)
    pooled = pooled.astype(BF16)
    projected = jnp.dot(pooled, enc_weight, preferred_element_type=F32)
    norm_scale = lax.rsqrt(jnp.mean(projected * projected, axis=1, keepdims=True) + 1e-06)
    encoded = (projected * norm_scale * enc_gain * width ** (-0.5)).astype(BF16)

    both = jnp.concatenate([encoded, swap_cores(encoded)])
    send_vectors = jnp.dot(to_slots, both, preferred_element_type=F32).astype(BF16)
    send_vectors = send_vectors.reshape(chips, 2 * label_cap, width)
    arrived = {k: to_chip(send_vectors[k], k) for k in others}
    got_vectors = jnp.concatenate([send_vectors[0]] + [arrived[k] for k in range(1, chips)])
    to_rows = (jnp.arange(slab_rows, dtype=I32)[:, None] == got_rows[None, :]).astype(BF16)
    delta = jnp.dot(to_rows, got_vectors, preferred_element_type=F32)
    head = (free_rows.astype(F32) + delta).astype(BF16)

    label_columns = lax.axis_index(ALL) * slab_rows + jnp.arange(slab_rows, dtype=I32)
    logits = lax.dot_general(all_docs, head, (((1,), (1,)), ((), ())), preferred_element_type=F32)
    hits = jnp.zeros(logits.shape, jnp.bool_)
    for column in range(pos_count):
        hits = hits | (all_positives[:, column : column + 1] == label_columns[None, :])
    errors = (jax.nn.sigmoid(logits) - hits.astype(F32)).astype(BF16)
    doc_terms = jnp.dot(errors, head, preferred_element_type=F32)
    doc_grad = jnp.sum(exchange(doc_terms.reshape(devices, own_docs, width), ALL), axis=0)
    picked = lax.dot_general(
        to_rows, errors, (((0,), (1,)), ((), ())), preferred_element_type=F32
    ).astype(BF16)
    picked = picked.reshape(chips, 2 * label_cap, all_count)
    arrived = {k: to_chip(picked[k], k) for k in others}
    returned = jnp.concatenate([picked[0]] + [arrived[k] for k in range(1, chips)])
    chip_errors = lax.dot_general(
        to_slots, returned, (((0,), (0,)), ((), ())), preferred_element_type=F32
    ).astype(BF16)
    ref_errors = chip_errors[:labels] + swap_cores(chip_errors[labels:])
    free_grad = lax.dot_general(
        errors, all_docs, (((0,), (0,)), ((), ())), preferred_element_type=F32
    ).astype(BF16)
    ref_grad = jnp.dot(ref_errors, all_docs, preferred_element_type=F32).astype(BF16)
    return (free_grad, doc_grad, ref_grad)


def on_device(token_table, enc_weight, enc_gain, label_tokens, *rest):
    shards = lax.axis_size("shard")
    labels, length = label_tokens.shape
    row_count = 5 * labels * length // 4
    plan = by_sums if shards % 2 == 0 and shards // 2 * labels < row_count else by_rows
    return plan(token_table, enc_weight, enc_gain, label_tokens, *rest)


def solution(mesh):
    in_specs = (
        P("shard", None),
        P(),
        P(),
        P(ALL, None),
        P(ALL, None),
        P(ALL),
        P(ALL, None),
        P(ALL, None),
        P(ALL, None),
    )
    out_specs = (P(ALL, None), P(ALL, None), P(ALL, None))
    return jax.shard_map(
        on_device, mesh=mesh, in_specs=in_specs, out_specs=out_specs, check_vma=False
    )
```

```python
import functools
import jax
import jax.numpy as jnp
from jax import lax
from jax.experimental import pallas as pl
from jax.experimental.pallas import tpu as pltpu
from jax.sharding import PartitionSpec as P

BF16 = jnp.bfloat16
F32 = jnp.float32
I32 = jnp.int32
ALL = ("grp", "shard")


def exchange(blocks, axes):
    return lax.all_to_all(blocks, axes, split_axis=0, concat_axis=0, tiled=True)


def inclusive_counts(marks):
    count = marks.shape[0]
    rows = lax.broadcasted_iota(I32, (count, count), 0)
    cols = lax.broadcasted_iota(I32, (count, count), 1)
    return jnp.dot((cols <= rows).astype(BF16), marks.astype(BF16), preferred_element_type=F32).astype(I32)


def token_places(owner, shards, cap):
    labels, length = owner.shape
    marks = (owner[:, :, None] == jnp.arange(shards, dtype=I32)).astype(I32)
    within = inclusive_counts(marks.reshape(labels, length * shards)).reshape(labels, length, shards)
    totals = within[-1]
    before = jnp.cumsum(totals, axis=0) - totals
    slot = jnp.sum((within + before[None] - 1) * marks, axis=2)
    return owner * cap + slot


def label_places(owner, shards, cap):
    marks = (owner[:, None] == jnp.arange(shards, dtype=I32)).astype(I32)
    slot = jnp.sum((inclusive_counts(marks) - 1) * marks, axis=1)
    return owner * cap + slot


def placed(values, places, size):
    hit = places[:, None] == jnp.arange(size, dtype=I32)[None, :]
    return jnp.sum(jnp.where(hit, values[:, None] + 1, 0), axis=0) - 1


def swap_cores(x):
    return lax.ppermute(x, "shard", [(i, i ^ 1) for i in range(lax.axis_size("shard"))])


def to_chip(x, k):
    return lax.ppermute(x, "shard", [(i, i ^ (2 * k)) for i in range(lax.axis_size("shard"))])


def by_rows(
    token_table, enc_weight, enc_gain, label_tokens, ref_owner, ref_row, free_rows, docs, positives
):
    shards = lax.axis_size("shard")
    devices = shards * lax.axis_size("grp")
    vocab_rows, width = token_table.shape
    labels, length = label_tokens.shape
    own_docs = docs.shape[0]
    pos_count = positives.shape[1]
    slab_rows = free_rows.shape[0]
    tokens = labels * length
    token_cap = 5 * tokens // (4 * shards)
    label_cap = 2 * labels // shards

    token_owner = label_tokens // vocab_rows
    token_dest = token_places(token_owner, shards, token_cap)
    send_ids = placed(
        (label_tokens - token_owner * vocab_rows).reshape(tokens),
        token_dest.reshape(tokens),
        shards * token_cap,
    )
    label_dest = label_places(ref_owner[:, 0], shards, label_cap)
    send_rows = placed(ref_row, label_dest, shards * label_cap)
    asked = exchange(
        jnp.concatenate(
            [send_ids.reshape(shards, token_cap), send_rows.reshape(shards, label_cap)], axis=1
        ),
        "shard",
    )
    got_rows = asked[:, token_cap:].reshape(shards * label_cap)

    digits = jnp.concatenate(
        [positives & 255, (positives >> 8) & 255, positives >> 16], axis=1
    ).astype(BF16)
    own_block = jnp.concatenate(
        [docs, digits, jnp.zeros((own_docs, 128 - 3 * pos_count), BF16)], axis=1
    )
    all_blocks = exchange(
        jnp.broadcast_to(own_block[None], (devices, own_docs, width + 128)), ALL
    ).reshape(devices * own_docs, width + 128)
    all_docs = all_blocks[:, :width]
    d = all_blocks[:, width : width + 3 * pos_count].astype(I32)
    all_positives = d[:, :pos_count] + 256 * d[:, pos_count : 2 * pos_count] + 65536 * d[:, 2 * pos_count :]

    found = token_table[jnp.maximum(asked[:, :token_cap], 0)]
    token_found = exchange(found, "shard").reshape(shards * token_cap, width)
    pick_tokens = jnp.zeros((labels, shards * token_cap), F32)
    for j in range(length):
        pick_tokens += (
            token_dest[:, j : j + 1] == jnp.arange(shards * token_cap, dtype=I32)[None, :]
        ).astype(F32)
    pooled = jnp.dot(
        (pick_tokens / length).astype(BF16), token_found, preferred_element_type=F32
    ).astype(BF16)
    projected = jnp.dot(pooled, enc_weight, preferred_element_type=F32)
    norm_scale = lax.rsqrt(jnp.mean(projected * projected, axis=1, keepdims=True) + 1e-06)
    encoded = (projected * norm_scale * enc_gain * width ** (-0.5)).astype(BF16)

    to_slots = (
        jnp.arange(shards * label_cap, dtype=I32)[:, None] == label_dest[None, :]
    ).astype(BF16)
    send_vectors = jnp.dot(to_slots, encoded, preferred_element_type=F32).astype(BF16)
    got_vectors = exchange(send_vectors.reshape(shards, label_cap, width), "shard").reshape(
        shards * label_cap, width
    )
    to_rows = (jnp.arange(slab_rows, dtype=I32)[:, None] == got_rows[None, :]).astype(BF16)
    delta = jnp.dot(to_rows, got_vectors, preferred_element_type=F32)
    head = (free_rows.astype(F32) + delta).astype(BF16)

    label_columns = lax.axis_index(ALL) * slab_rows + jnp.arange(slab_rows, dtype=I32)
    logits = lax.dot_general(all_docs, head, (((1,), (1,)), ((), ())), preferred_element_type=F32)
    hits = jnp.zeros(logits.shape, jnp.bool_)
    for column in range(pos_count):
        hits = hits | (all_positives[:, column : column + 1] == label_columns[None, :])
    errors = (jax.nn.sigmoid(logits) - hits.astype(F32)).astype(BF16)
    doc_terms = jnp.dot(errors, head, preferred_element_type=F32)
    free_grad = lax.dot_general(
        errors, all_docs, (((0,), (0,)), ((), ())), preferred_element_type=F32
    ).astype(BF16)
    picked = lax.dot_general(
        to_rows, errors, (((0,), (1,)), ((), ())), preferred_element_type=F32
    ).astype(BF16)
    returned = exchange(picked.reshape(shards, label_cap, devices * own_docs), "shard").reshape(
        shards * label_cap, devices * own_docs
    )
    ref_errors = lax.dot_general(
        to_slots, returned, (((0,), (0,)), ((), ())), preferred_element_type=F32
    ).astype(BF16)
    ref_grad = jnp.dot(ref_errors, all_docs, preferred_element_type=F32).astype(BF16)
    doc_grad = jnp.sum(exchange(doc_terms.reshape(devices, own_docs, width), ALL), axis=0)
    return (free_grad, doc_grad, ref_grad)


LANES = 128
SUBLANES = 8
PIECES = 4


def sum_kernel(length, starts_ref, near_ref, far_ref, *refs):
    outs, (stage, rows, sums, sems) = refs[:-4], refs[-4:]
    vocab_rows, width = near_ref.shape
    chunks = width // LANES
    tile = SUBLANES * chunks
    labels = outs[0].shape[0]
    piece = vocab_rows // PIECES

    copies = []
    for half, table in enumerate((near_ref, far_ref)):
        for p in range(PIECES):
            at = half * PIECES + p
            copies.append(
                pltpu.make_async_copy(
                    table.at[pl.ds(p * piece, piece)], stage.at[pl.ds(at * piece, piece)], sems.at[at]
                )
            )
    for copy in copies:
        copy.start()
    rows[pl.ds(2 * vocab_rows * chunks, tile), :] = jnp.zeros((tile, LANES), F32)
    for at, copy in enumerate(copies):
        copy.wait()

        @pl.loop(0, piece // 16, unroll=4)
        def _(group):
            first = pl.multiple_of(at * piece + group * 16, 16)
            block = stage[pl.ds(first, 16), :].astype(F32)
            to = pl.multiple_of(first * chunks, 16)
            for h in range(2):
                for c in range(chunks):
                    rows[pl.ds(to + h * tile + c * SUBLANES, SUBLANES), :] = block[
                        h * SUBLANES : (h + 1) * SUBLANES, c * LANES : (c + 1) * LANES
                    ]

    @pl.loop(0, len(outs) * labels // SUBLANES)
    def _(group):
        for q in range(SUBLANES):
            first = (group * SUBLANES + q) * length
            terms = [
                rows[pl.ds(starts_ref[first + j], chunks, stride=SUBLANES), :] for j in range(length)
            ]
            while len(terms) > 1:
                terms = [a + b for a, b in zip(terms[::2], terms[1::2])] + terms[len(terms) // 2 * 2 :]
            sums[pl.ds(group * tile + q, chunks, stride=SUBLANES), :] = terms[0] / length

    for n, out in enumerate(outs):
        for group in range(labels // 16):
            for c in range(chunks):
                at = ((n * labels) // SUBLANES + 2 * group) * tile + c * SUBLANES
                out[16 * group : 16 * group + 16, c * LANES : (c + 1) * LANES] = jnp.concatenate(
                    [sums[at : at + SUBLANES, :], sums[at + tile : at + tile + SUBLANES, :]]
                ).astype(out.dtype)


def partial_means(starts, near, far, labels, length, kinds):
    vocab_rows, width = near.shape
    chunks = width // LANES
    return pl.pallas_call(
        functools.partial(sum_kernel, length),
        out_shape=[jax.ShapeDtypeStruct((labels, width), kind) for kind in kinds],
        in_specs=[
            pl.BlockSpec(memory_space=pltpu.SMEM),
            pl.BlockSpec(memory_space=pl.ANY),
            pl.BlockSpec(memory_space=pl.ANY),
        ],
        out_specs=[pl.BlockSpec(memory_space=pltpu.VMEM) for _ in kinds],
        scratch_shapes=[
            pltpu.VMEM((2 * vocab_rows, width), BF16),
            pltpu.VMEM(((2 * vocab_rows + 2 * SUBLANES) * chunks, LANES), F32),
            pltpu.VMEM(((len(kinds) * labels + SUBLANES) * chunks, LANES), F32),
            pltpu.SemaphoreType.DMA((2 * PIECES,)),
        ],
        compiler_params=pltpu.CompilerParams(vmem_limit_bytes=56 * 1024 * 1024),
        cost_estimate=pl.CostEstimate(
            flops=len(kinds) * labels * length * width,
            bytes_accessed=4 * vocab_rows * width,
            transcendentals=0,
        ),
    )(starts, near, far)


def by_sums(
    token_table, enc_weight, enc_gain, label_tokens, ref_owner, ref_row, free_rows, docs, positives
):
    shards = lax.axis_size("shard")
    chips = shards // 2
    devices = shards * lax.axis_size("grp")
    me = lax.axis_index("shard")
    vocab_rows, width = token_table.shape
    labels, length = label_tokens.shape
    own_docs = docs.shape[0]
    all_count = devices * own_docs
    pos_count = positives.shape[1]
    slab_rows = free_rows.shape[0]
    tokens = labels * length
    label_cap = 2 * labels // shards
    others = [k for k in range(chips - 1, 0, -1)]

    other_table = swap_cores(token_table)

    asked = {k: to_chip(label_tokens, k) for k in others}
    asked[0] = label_tokens

    label_dest = label_places(ref_owner[:, 0] ^ me, shards, label_cap)
    mine = jnp.stack([label_dest, ref_row])
    theirs = swap_cores(mine)
    own_rel = label_dest // label_cap
    other_rel = theirs[0] // label_cap
    places = jnp.concatenate(
        [
            jnp.where(own_rel % 2 == 0, label_dest, -1),
            jnp.where(other_rel % 2 == 1, theirs[0], -1),
        ]
    )
    slots = shards * label_cap
    to_slots = jnp.arange(slots, dtype=I32)[:, None] == places[None, :]
    chip_rows = jnp.concatenate([ref_row, theirs[1]])
    send_rows = jnp.sum(jnp.where(to_slots, chip_rows[None, :] + 1, 0), axis=1) - 1
    send_rows = send_rows.reshape(chips, 2 * label_cap)
    to_slots = to_slots.astype(BF16)
    got_rows = jnp.concatenate(
        [send_rows[0:1]] + [to_chip(send_rows[k : k + 1], k) for k in range(1, chips)]
    ).reshape(slots)

    digits = jnp.concatenate(
        [positives & 255, (positives >> 8) & 255, positives >> 16], axis=1
    ).astype(BF16)
    own_block = jnp.concatenate(
        [docs, digits, jnp.zeros((own_docs, 128 - 3 * pos_count), BF16)], axis=1
    )
    all_blocks = exchange(
        jnp.broadcast_to(own_block[None], (devices, own_docs, width + 128)), ALL
    ).reshape(all_count, width + 128)
    all_docs = all_blocks[:, :width]
    d = all_blocks[:, width : width + 3 * pos_count].astype(I32)
    all_positives = d[:, :pos_count] + 256 * d[:, pos_count : 2 * pos_count] + 65536 * d[:, 2 * pos_count :]

    def starts(ks):
        ids = jnp.concatenate([asked[k] for k in ks])
        near = ids - me * vocab_rows
        far = ids - (me ^ 1) * vocab_rows
        row = jnp.where(
            (near >= 0) & (near < vocab_rows),
            near,
            jnp.where((far >= 0) & (far < vocab_rows), far + vocab_rows, 2 * vocab_rows),
        )
        first = (row // SUBLANES) * (SUBLANES * (width // LANES)) + row % SUBLANES
        return first.reshape(len(ks) * tokens)

    sent = []
    half = len(others) - len(others) // 3
    for ks in (others[:half], others[half:] + [0]):
        sent += partial_means(
            starts(ks), token_table, other_table, labels, length, [BF16 if k else F32 for k in ks]
        )
    arrived = [to_chip(term, k) for term, k in zip(sent, others)]
    pooled = sent[-1]
    for term in arrived:
        pooled = pooled + term.astype(F32)
    pooled = pooled.astype(BF16)
    projected = jnp.dot(pooled, enc_weight, preferred_element_type=F32)
    norm_scale = lax.rsqrt(jnp.mean(projected * projected, axis=1, keepdims=True) + 1e-06)
    encoded = (projected * norm_scale * enc_gain * width ** (-0.5)).astype(BF16)

    both = jnp.concatenate([encoded, swap_cores(encoded)])
    send_vectors = jnp.dot(to_slots, both, preferred_element_type=F32).astype(BF16)
    send_vectors = send_vectors.reshape(chips, 2 * label_cap, width)
    arrived = {k: to_chip(send_vectors[k], k) for k in others}
    got_vectors = jnp.concatenate([send_vectors[0]] + [arrived[k] for k in range(1, chips)])
    to_rows = (jnp.arange(slab_rows, dtype=I32)[:, None] == got_rows[None, :]).astype(BF16)
    delta = jnp.dot(to_rows, got_vectors, preferred_element_type=F32)
    head = (free_rows.astype(F32) + delta).astype(BF16)

    label_columns = lax.axis_index(ALL) * slab_rows + jnp.arange(slab_rows, dtype=I32)
    logits = lax.dot_general(all_docs, head, (((1,), (1,)), ((), ())), preferred_element_type=F32)
    hits = jnp.zeros(logits.shape, jnp.bool_)
    for column in range(pos_count):
        hits = hits | (all_positives[:, column : column + 1] == label_columns[None, :])
    errors = (jax.nn.sigmoid(logits) - hits.astype(F32)).astype(BF16)
    doc_terms = jnp.dot(errors, head, preferred_element_type=F32)
    doc_grad = jnp.sum(exchange(doc_terms.reshape(devices, own_docs, width), ALL), axis=0)
    picked = lax.dot_general(
        to_rows, errors, (((0,), (1,)), ((), ())), preferred_element_type=F32
    ).astype(BF16)
    picked = picked.reshape(chips, 2 * label_cap, all_count)
    arrived = {k: to_chip(picked[k], k) for k in others}
    returned = jnp.concatenate([picked[0]] + [arrived[k] for k in range(1, chips)])
    chip_errors = lax.dot_general(
        to_slots, returned, (((0,), (0,)), ((), ())), preferred_element_type=F32
    ).astype(BF16)
    ref_errors = chip_errors[:labels] + swap_cores(chip_errors[labels:])
    free_grad = lax.dot_general(
        errors, all_docs, (((0,), (0,)), ((), ())), preferred_element_type=F32
    ).astype(BF16)
    ref_grad = jnp.dot(ref_errors, all_docs, preferred_element_type=F32).astype(BF16)
    return (free_grad, doc_grad, ref_grad)


def on_device(token_table, enc_weight, enc_gain, label_tokens, *rest):
    shards = lax.axis_size("shard")
    labels, length = label_tokens.shape
    row_count = 5 * labels * length // 4
    plan = by_sums if shards % 2 == 0 and shards // 2 * labels < row_count else by_rows
    return plan(token_table, enc_weight, enc_gain, label_tokens, *rest)


def solution(mesh):
    in_specs = (
        P("shard", None),
        P(),
        P(),
        P(ALL, None),
        P(ALL, None),
        P(ALL),
        P(ALL, None),
        P(ALL, None),
        P(ALL, None),
    )
    out_specs = (P(ALL, None), P(ALL, None), P(ALL, None))
    return jax.shard_map(
        on_device, mesh=mesh, in_specs=in_specs, out_specs=out_specs, check_vma=False
    )
```

```python
import functools
import jax
import jax.numpy as jnp
from jax import lax
from jax.experimental import pallas as pl
from jax.experimental.pallas import tpu as pltpu
from jax.sharding import PartitionSpec as P

BF16 = jnp.bfloat16
F32 = jnp.float32
I32 = jnp.int32
ALL = ("grp", "shard")


def exchange(blocks, axes):
    return lax.all_to_all(blocks, axes, split_axis=0, concat_axis=0, tiled=True)


def inclusive_counts(marks):
    count = marks.shape[0]
    rows = lax.broadcasted_iota(I32, (count, count), 0)
    cols = lax.broadcasted_iota(I32, (count, count), 1)
    return jnp.dot((cols <= rows).astype(BF16), marks.astype(BF16), preferred_element_type=F32).astype(I32)


def token_places(owner, shards, cap):
    labels, length = owner.shape
    marks = (owner[:, :, None] == jnp.arange(shards, dtype=I32)).astype(I32)
    within = inclusive_counts(marks.reshape(labels, length * shards)).reshape(labels, length, shards)
    totals = within[-1]
    before = jnp.cumsum(totals, axis=0) - totals
    slot = jnp.sum((within + before[None] - 1) * marks, axis=2)
    return owner * cap + slot


def label_places(owner, shards, cap):
    marks = (owner[:, None] == jnp.arange(shards, dtype=I32)).astype(I32)
    slot = jnp.sum((inclusive_counts(marks) - 1) * marks, axis=1)
    return owner * cap + slot


def placed(values, places, size):
    hit = places[:, None] == jnp.arange(size, dtype=I32)[None, :]
    return jnp.sum(jnp.where(hit, values[:, None] + 1, 0), axis=0) - 1


def swap_cores(x):
    return lax.ppermute(x, "shard", [(i, i ^ 1) for i in range(lax.axis_size("shard"))])


def to_chip(x, k):
    return lax.ppermute(x, "shard", [(i, i ^ (2 * k)) for i in range(lax.axis_size("shard"))])


def by_rows(
    token_table, enc_weight, enc_gain, label_tokens, ref_owner, ref_row, free_rows, docs, positives
):
    shards = lax.axis_size("shard")
    devices = shards * lax.axis_size("grp")
    vocab_rows, width = token_table.shape
    labels, length = label_tokens.shape
    own_docs = docs.shape[0]
    pos_count = positives.shape[1]
    slab_rows = free_rows.shape[0]
    tokens = labels * length
    token_cap = 5 * tokens // (4 * shards)
    label_cap = 2 * labels // shards

    token_owner = label_tokens // vocab_rows
    token_dest = token_places(token_owner, shards, token_cap)
    send_ids = placed(
        (label_tokens - token_owner * vocab_rows).reshape(tokens),
        token_dest.reshape(tokens),
        shards * token_cap,
    )
    label_dest = label_places(ref_owner[:, 0], shards, label_cap)
    send_rows = placed(ref_row, label_dest, shards * label_cap)
    asked = exchange(
        jnp.concatenate(
            [send_ids.reshape(shards, token_cap), send_rows.reshape(shards, label_cap)], axis=1
        ),
        "shard",
    )
    got_rows = asked[:, token_cap:].reshape(shards * label_cap)

    digits = jnp.concatenate(
        [positives & 255, (positives >> 8) & 255, positives >> 16], axis=1
    ).astype(BF16)
    own_block = jnp.concatenate(
        [docs, digits, jnp.zeros((own_docs, 128 - 3 * pos_count), BF16)], axis=1
    )
    all_blocks = exchange(
        jnp.broadcast_to(own_block[None], (devices, own_docs, width + 128)), ALL
    ).reshape(devices * own_docs, width + 128)
    all_docs = all_blocks[:, :width]
    d = all_blocks[:, width : width + 3 * pos_count].astype(I32)
    all_positives = d[:, :pos_count] + 256 * d[:, pos_count : 2 * pos_count] + 65536 * d[:, 2 * pos_count :]

    found = token_table[jnp.maximum(asked[:, :token_cap], 0)]
    token_found = exchange(found, "shard").reshape(shards * token_cap, width)
    pick_tokens = jnp.zeros((labels, shards * token_cap), F32)
    for j in range(length):
        pick_tokens += (
            token_dest[:, j : j + 1] == jnp.arange(shards * token_cap, dtype=I32)[None, :]
        ).astype(F32)
    pooled = jnp.dot(
        (pick_tokens / length).astype(BF16), token_found, preferred_element_type=F32
    ).astype(BF16)
    projected = jnp.dot(pooled, enc_weight, preferred_element_type=F32)
    norm_scale = lax.rsqrt(jnp.mean(projected * projected, axis=1, keepdims=True) + 1e-06)
    encoded = (projected * norm_scale * enc_gain * width ** (-0.5)).astype(BF16)

    to_slots = (
        jnp.arange(shards * label_cap, dtype=I32)[:, None] == label_dest[None, :]
    ).astype(BF16)
    send_vectors = jnp.dot(to_slots, encoded, preferred_element_type=F32).astype(BF16)
    got_vectors = exchange(send_vectors.reshape(shards, label_cap, width), "shard").reshape(
        shards * label_cap, width
    )
    to_rows = (jnp.arange(slab_rows, dtype=I32)[:, None] == got_rows[None, :]).astype(BF16)
    delta = jnp.dot(to_rows, got_vectors, preferred_element_type=F32)
    head = (free_rows.astype(F32) + delta).astype(BF16)

    label_columns = lax.axis_index(ALL) * slab_rows + jnp.arange(slab_rows, dtype=I32)
    logits = lax.dot_general(all_docs, head, (((1,), (1,)), ((), ())), preferred_element_type=F32)
    hits = jnp.zeros(logits.shape, jnp.bool_)
    for column in range(pos_count):
        hits = hits | (all_positives[:, column : column + 1] == label_columns[None, :])
    errors = (jax.nn.sigmoid(logits) - hits.astype(F32)).astype(BF16)
    doc_terms = jnp.dot(errors, head, preferred_element_type=F32)
    free_grad = lax.dot_general(
        errors, all_docs, (((0,), (0,)), ((), ())), preferred_element_type=F32
    ).astype(BF16)
    picked = lax.dot_general(
        to_rows, errors, (((0,), (1,)), ((), ())), preferred_element_type=F32
    ).astype(BF16)
    returned = exchange(picked.reshape(shards, label_cap, devices * own_docs), "shard").reshape(
        shards * label_cap, devices * own_docs
    )
    ref_errors = lax.dot_general(
        to_slots, returned, (((0,), (0,)), ((), ())), preferred_element_type=F32
    ).astype(BF16)
    ref_grad = jnp.dot(ref_errors, all_docs, preferred_element_type=F32).astype(BF16)
    doc_grad = jnp.sum(exchange(doc_terms.reshape(devices, own_docs, width), ALL), axis=0)
    return (free_grad, doc_grad, ref_grad)


LANES = 128
SUBLANES = 8
PIECES = 4


def sum_kernel(length, starts_ref, near_ref, far_ref, *refs):
    outs, (stage, rows, sums, sems) = refs[:-4], refs[-4:]
    vocab_rows, width = near_ref.shape
    chunks = width // LANES
    tile = SUBLANES * chunks
    labels = outs[0].shape[0]
    piece = vocab_rows // PIECES

    copies = []
    for half, table in enumerate((near_ref, far_ref)):
        for p in range(PIECES):
            at = half * PIECES + p
            copies.append(
                pltpu.make_async_copy(
                    table.at[pl.ds(p * piece, piece)], stage.at[pl.ds(at * piece, piece)], sems.at[at]
                )
            )
    for copy in copies:
        copy.start()
    rows[pl.ds(2 * vocab_rows * chunks, tile), :] = jnp.zeros((tile, LANES), F32)
    for at, copy in enumerate(copies):
        copy.wait()

        @pl.loop(0, piece // 16, unroll=4)
        def _(group):
            first = pl.multiple_of(at * piece + group * 16, 16)
            block = stage[pl.ds(first, 16), :].astype(F32)
            to = pl.multiple_of(first * chunks, 16)
            for h in range(2):
                for c in range(chunks):
                    rows[pl.ds(to + h * tile + c * SUBLANES, SUBLANES), :] = block[
                        h * SUBLANES : (h + 1) * SUBLANES, c * LANES : (c + 1) * LANES
                    ]

    @pl.loop(0, len(outs) * labels // SUBLANES)
    def _(group):
        for q in range(SUBLANES):
            first = (group * SUBLANES + q) * length
            terms = [
                rows[pl.ds(starts_ref[first + j], chunks, stride=SUBLANES), :] for j in range(length)
            ]
            while len(terms) > 1:
                terms = [a + b for a, b in zip(terms[::2], terms[1::2])] + terms[len(terms) // 2 * 2 :]
            sums[pl.ds(group * tile + q, chunks, stride=SUBLANES), :] = terms[0] / length

    for n, out in enumerate(outs):
        for group in range(labels // 16):
            for c in range(chunks):
                at = ((n * labels) // SUBLANES + 2 * group) * tile + c * SUBLANES
                out[16 * group : 16 * group + 16, c * LANES : (c + 1) * LANES] = jnp.concatenate(
                    [sums[at : at + SUBLANES, :], sums[at + tile : at + tile + SUBLANES, :]]
                ).astype(out.dtype)


def partial_means(starts, near, far, labels, length, kinds):
    vocab_rows, width = near.shape
    chunks = width // LANES
    return pl.pallas_call(
        functools.partial(sum_kernel, length),
        out_shape=[jax.ShapeDtypeStruct((labels, width), kind) for kind in kinds],
        in_specs=[
            pl.BlockSpec(memory_space=pltpu.SMEM),
            pl.BlockSpec(memory_space=pl.ANY),
            pl.BlockSpec(memory_space=pl.ANY),
        ],
        out_specs=[pl.BlockSpec(memory_space=pltpu.VMEM) for _ in kinds],
        scratch_shapes=[
            pltpu.VMEM((2 * vocab_rows, width), BF16),
            pltpu.VMEM(((2 * vocab_rows + 2 * SUBLANES) * chunks, LANES), F32),
            pltpu.VMEM(((len(kinds) * labels + SUBLANES) * chunks, LANES), F32),
            pltpu.SemaphoreType.DMA((2 * PIECES,)),
        ],
        compiler_params=pltpu.CompilerParams(vmem_limit_bytes=56 * 1024 * 1024),
        cost_estimate=pl.CostEstimate(
            flops=len(kinds) * labels * length * width,
            bytes_accessed=4 * vocab_rows * width,
            transcendentals=0,
        ),
    )(starts, near, far)


def by_sums(
    token_table, enc_weight, enc_gain, label_tokens, ref_owner, ref_row, free_rows, docs, positives
):
    shards = lax.axis_size("shard")
    chips = shards // 2
    devices = shards * lax.axis_size("grp")
    me = lax.axis_index("shard")
    vocab_rows, width = token_table.shape
    labels, length = label_tokens.shape
    own_docs = docs.shape[0]
    all_count = devices * own_docs
    pos_count = positives.shape[1]
    slab_rows = free_rows.shape[0]
    tokens = labels * length
    label_cap = 2 * labels // shards
    others = [k for k in range(chips - 1, 0, -1)]

    other_table = swap_cores(token_table)

    asked = {k: to_chip(label_tokens, k) for k in others}
    asked[0] = label_tokens

    def starts(ks):
        ids = jnp.concatenate([asked[k] for k in ks])
        near = ids - me * vocab_rows
        far = ids - (me ^ 1) * vocab_rows
        row = jnp.where(
            (near >= 0) & (near < vocab_rows),
            near,
            jnp.where((far >= 0) & (far < vocab_rows), far + vocab_rows, 2 * vocab_rows),
        )
        first = (row // SUBLANES) * (SUBLANES * (width // LANES)) + row % SUBLANES
        return first.reshape(len(ks) * tokens)

    ks = others + [0]
    sent = partial_means(
        starts(ks), token_table, other_table, labels, length, [BF16 if k else F32 for k in ks]
    )
    arrived = [to_chip(term, k) for term, k in zip(sent, others)]
    docs, positives, ref_owner, ref_row, own = lax.optimization_barrier(
        (docs, positives, ref_owner, ref_row, sent[-1])
    )

    label_dest = label_places(ref_owner[:, 0] ^ me, shards, label_cap)
    mine = jnp.stack([label_dest, ref_row])
    theirs = swap_cores(mine)
    own_rel = label_dest // label_cap
    other_rel = theirs[0] // label_cap
    places = jnp.concatenate(
        [
            jnp.where(own_rel % 2 == 0, label_dest, -1),
            jnp.where(other_rel % 2 == 1, theirs[0], -1),
        ]
    )
    slots = shards * label_cap
    to_slots = jnp.arange(slots, dtype=I32)[:, None] == places[None, :]
    chip_rows = jnp.concatenate([ref_row, theirs[1]])
    send_rows = jnp.sum(jnp.where(to_slots, chip_rows[None, :] + 1, 0), axis=1) - 1
    send_rows = send_rows.reshape(chips, 2 * label_cap)
    to_slots = to_slots.astype(BF16)
    got_rows = jnp.concatenate(
        [send_rows[0:1]] + [to_chip(send_rows[k : k + 1], k) for k in range(1, chips)]
    ).reshape(slots)

    digits = jnp.concatenate(
        [positives & 255, (positives >> 8) & 255, positives >> 16], axis=1
    ).astype(BF16)
    own_block = jnp.concatenate(
        [docs, digits, jnp.zeros((own_docs, 128 - 3 * pos_count), BF16)], axis=1
    )
    all_blocks = exchange(
        jnp.broadcast_to(own_block[None], (devices, own_docs, width + 128)), ALL
    ).reshape(all_count, width + 128)
    all_docs = all_blocks[:, :width]
    d = all_blocks[:, width : width + 3 * pos_count].astype(I32)
    all_positives = d[:, :pos_count] + 256 * d[:, pos_count : 2 * pos_count] + 65536 * d[:, 2 * pos_count :]

    pooled = own
    for term in arrived:
        pooled = pooled + term.astype(F32)
    pooled = pooled.astype(BF16)
    projected = jnp.dot(pooled, enc_weight, preferred_element_type=F32)
    norm_scale = lax.rsqrt(jnp.mean(projected * projected, axis=1, keepdims=True) + 1e-06)
    encoded = (projected * norm_scale * enc_gain * width ** (-0.5)).astype(BF16)

    both = jnp.concatenate([encoded, swap_cores(encoded)])
    send_vectors = jnp.dot(to_slots, both, preferred_element_type=F32).astype(BF16)
    send_vectors = send_vectors.reshape(chips, 2 * label_cap, width)
    arrived = {k: to_chip(send_vectors[k], k) for k in others}
    got_vectors = jnp.concatenate([send_vectors[0]] + [arrived[k] for k in range(1, chips)])
    to_rows = (jnp.arange(slab_rows, dtype=I32)[:, None] == got_rows[None, :]).astype(BF16)
    delta = jnp.dot(to_rows, got_vectors, preferred_element_type=F32)
    head = (free_rows.astype(F32) + delta).astype(BF16)

    label_columns = lax.axis_index(ALL) * slab_rows + jnp.arange(slab_rows, dtype=I32)
    logits = lax.dot_general(all_docs, head, (((1,), (1,)), ((), ())), preferred_element_type=F32)
    hits = jnp.zeros(logits.shape, jnp.bool_)
    for column in range(pos_count):
        hits = hits | (all_positives[:, column : column + 1] == label_columns[None, :])
    errors = (jax.nn.sigmoid(logits) - hits.astype(F32)).astype(BF16)
    doc_terms = jnp.dot(errors, head, preferred_element_type=F32)
    doc_terms = doc_terms.reshape(devices, own_docs, width)
    doc_terms, late_errors = lax.optimization_barrier((doc_terms, errors))
    doc_grad = jnp.sum(exchange(doc_terms, ALL), axis=0)
    picked = lax.dot_general(
        to_rows, late_errors, (((0,), (1,)), ((), ())), preferred_element_type=F32
    ).astype(BF16)
    picked = picked.reshape(chips, 2 * label_cap, all_count)
    arrived = {k: to_chip(picked[k], k) for k in others}
    returned = jnp.concatenate([picked[0]] + [arrived[k] for k in range(1, chips)])
    chip_errors = lax.dot_general(
        to_slots, returned, (((0,), (0,)), ((), ())), preferred_element_type=F32
    ).astype(BF16)
    ref_errors = chip_errors[:labels] + swap_cores(chip_errors[labels:])
    free_grad = lax.dot_general(
        errors, all_docs, (((0,), (0,)), ((), ())), preferred_element_type=F32
    ).astype(BF16)
    ref_grad = jnp.dot(ref_errors, all_docs, preferred_element_type=F32).astype(BF16)
    return (free_grad, doc_grad, ref_grad)


def on_device(token_table, enc_weight, enc_gain, label_tokens, *rest):
    shards = lax.axis_size("shard")
    labels, length = label_tokens.shape
    row_count = 5 * labels * length // 4
    plan = by_sums if shards % 2 == 0 and shards // 2 * labels < row_count else by_rows
    return plan(token_table, enc_weight, enc_gain, label_tokens, *rest)


def solution(mesh):
    in_specs = (
        P("shard", None),
        P(),
        P(),
        P(ALL, None),
        P(ALL, None),
        P(ALL),
        P(ALL, None),
        P(ALL, None),
        P(ALL, None),
    )
    out_specs = (P(ALL, None), P(ALL, None), P(ALL, None))
    return jax.shard_map(
        on_device, mesh=mesh, in_specs=in_specs, out_specs=out_specs, check_vma=False
    )
```

```python
import functools
import jax
import jax.numpy as jnp
from jax import lax
from jax.experimental import pallas as pl
from jax.experimental.pallas import tpu as pltpu
from jax.sharding import PartitionSpec as P

BF16 = jnp.bfloat16
F32 = jnp.float32
I32 = jnp.int32
ALL = ("grp", "shard")


def exchange(blocks, axes):
    return lax.all_to_all(blocks, axes, split_axis=0, concat_axis=0, tiled=True)


def inclusive_counts(marks):
    count = marks.shape[0]
    rows = lax.broadcasted_iota(I32, (count, count), 0)
    cols = lax.broadcasted_iota(I32, (count, count), 1)
    return jnp.dot((cols <= rows).astype(BF16), marks.astype(BF16), preferred_element_type=F32).astype(I32)


def token_places(owner, shards, cap):
    labels, length = owner.shape
    marks = (owner[:, :, None] == jnp.arange(shards, dtype=I32)).astype(I32)
    within = inclusive_counts(marks.reshape(labels, length * shards)).reshape(labels, length, shards)
    totals = within[-1]
    before = jnp.cumsum(totals, axis=0) - totals
    slot = jnp.sum((within + before[None] - 1) * marks, axis=2)
    return owner * cap + slot


def label_places(owner, shards, cap):
    marks = (owner[:, None] == jnp.arange(shards, dtype=I32)).astype(I32)
    slot = jnp.sum((inclusive_counts(marks) - 1) * marks, axis=1)
    return owner * cap + slot


def placed(values, places, size):
    hit = places[:, None] == jnp.arange(size, dtype=I32)[None, :]
    return jnp.sum(jnp.where(hit, values[:, None] + 1, 0), axis=0) - 1


def swap_cores(x):
    return lax.ppermute(x, "shard", [(i, i ^ 1) for i in range(lax.axis_size("shard"))])


def to_chip(x, k):
    return lax.ppermute(x, "shard", [(i, i ^ (2 * k)) for i in range(lax.axis_size("shard"))])


def by_rows(
    token_table, enc_weight, enc_gain, label_tokens, ref_owner, ref_row, free_rows, docs, positives
):
    shards = lax.axis_size("shard")
    devices = shards * lax.axis_size("grp")
    vocab_rows, width = token_table.shape
    labels, length = label_tokens.shape
    own_docs = docs.shape[0]
    pos_count = positives.shape[1]
    slab_rows = free_rows.shape[0]
    tokens = labels * length
    token_cap = 5 * tokens // (4 * shards)
    label_cap = 2 * labels // shards

    token_owner = label_tokens // vocab_rows
    token_dest = token_places(token_owner, shards, token_cap)
    send_ids = placed(
        (label_tokens - token_owner * vocab_rows).reshape(tokens),
        token_dest.reshape(tokens),
        shards * token_cap,
    )
    label_dest = label_places(ref_owner[:, 0], shards, label_cap)
    send_rows = placed(ref_row, label_dest, shards * label_cap)
    asked = exchange(
        jnp.concatenate(
            [send_ids.reshape(shards, token_cap), send_rows.reshape(shards, label_cap)], axis=1
        ),
        "shard",
    )
    got_rows = asked[:, token_cap:].reshape(shards * label_cap)

    digits = jnp.concatenate(
        [positives & 255, (positives >> 8) & 255, positives >> 16], axis=1
    ).astype(BF16)
    own_block = jnp.concatenate(
        [docs, digits, jnp.zeros((own_docs, 128 - 3 * pos_count), BF16)], axis=1
    )
    all_blocks = exchange(
        jnp.broadcast_to(own_block[None], (devices, own_docs, width + 128)), ALL
    ).reshape(devices * own_docs, width + 128)
    all_docs = all_blocks[:, :width]
    d = all_blocks[:, width : width + 3 * pos_count].astype(I32)
    all_positives = d[:, :pos_count] + 256 * d[:, pos_count : 2 * pos_count] + 65536 * d[:, 2 * pos_count :]

    found = token_table[jnp.maximum(asked[:, :token_cap], 0)]
    token_found = exchange(found, "shard").reshape(shards * token_cap, width)
    pick_tokens = jnp.zeros((labels, shards * token_cap), F32)
    for j in range(length):
        pick_tokens += (
            token_dest[:, j : j + 1] == jnp.arange(shards * token_cap, dtype=I32)[None, :]
        ).astype(F32)
    pooled = jnp.dot(
        (pick_tokens / length).astype(BF16), token_found, preferred_element_type=F32
    ).astype(BF16)
    projected = jnp.dot(pooled, enc_weight, preferred_element_type=F32)
    norm_scale = lax.rsqrt(jnp.mean(projected * projected, axis=1, keepdims=True) + 1e-06)
    encoded = (projected * norm_scale * enc_gain * width ** (-0.5)).astype(BF16)

    to_slots = (
        jnp.arange(shards * label_cap, dtype=I32)[:, None] == label_dest[None, :]
    ).astype(BF16)
    send_vectors = jnp.dot(to_slots, encoded, preferred_element_type=F32).astype(BF16)
    got_vectors = exchange(send_vectors.reshape(shards, label_cap, width), "shard").reshape(
        shards * label_cap, width
    )
    to_rows = (jnp.arange(slab_rows, dtype=I32)[:, None] == got_rows[None, :]).astype(BF16)
    delta = jnp.dot(to_rows, got_vectors, preferred_element_type=F32)
    head = (free_rows.astype(F32) + delta).astype(BF16)

    label_columns = lax.axis_index(ALL) * slab_rows + jnp.arange(slab_rows, dtype=I32)
    logits = lax.dot_general(all_docs, head, (((1,), (1,)), ((), ())), preferred_element_type=F32)
    hits = jnp.zeros(logits.shape, jnp.bool_)
    for column in range(pos_count):
        hits = hits | (all_positives[:, column : column + 1] == label_columns[None, :])
    errors = (jax.nn.sigmoid(logits) - hits.astype(F32)).astype(BF16)
    doc_terms = jnp.dot(errors, head, preferred_element_type=F32)
    free_grad = lax.dot_general(
        errors, all_docs, (((0,), (0,)), ((), ())), preferred_element_type=F32
    ).astype(BF16)
    picked = lax.dot_general(
        to_rows, errors, (((0,), (1,)), ((), ())), preferred_element_type=F32
    ).astype(BF16)
    returned = exchange(picked.reshape(shards, label_cap, devices * own_docs), "shard").reshape(
        shards * label_cap, devices * own_docs
    )
    ref_errors = lax.dot_general(
        to_slots, returned, (((0,), (0,)), ((), ())), preferred_element_type=F32
    ).astype(BF16)
    ref_grad = jnp.dot(ref_errors, all_docs, preferred_element_type=F32).astype(BF16)
    doc_grad = jnp.sum(exchange(doc_terms.reshape(devices, own_docs, width), ALL), axis=0)
    return (free_grad, doc_grad, ref_grad)


LANES = 128
SUBLANES = 8
PIECES = 4


def sum_kernel(length, held, starts_ref, near_ref, far_ref, *refs):
    moved = held - 1 if held else 0
    refs = refs[1:] if held else refs
    sources, refs, targets, note, (stage, rows, sums, sems) = (
        refs[:moved], refs[moved : -5 - moved], refs[len(refs) - 5 - moved : -5], refs[-5], refs[-4:]
    )
    outs = refs
    note[...] = jnp.zeros(note.shape, F32)
    moves = [
        pltpu.make_async_copy(a, b, sems.at[2 * PIECES + n])
        for n, (a, b) in enumerate(zip(sources, targets))
    ]
    vocab_rows, width = near_ref.shape
    chunks = width // LANES
    tile = SUBLANES * chunks
    labels = outs[0].shape[0]
    piece = vocab_rows // PIECES

    copies = []
    for half, table in enumerate((near_ref, far_ref)):
        for p in range(PIECES):
            at = half * PIECES + p
            copies.append(
                pltpu.make_async_copy(
                    table.at[pl.ds(p * piece, piece)], stage.at[pl.ds(at * piece, piece)], sems.at[at]
                )
            )
    for copy in copies + moves:
        copy.start()
    rows[pl.ds(2 * vocab_rows * chunks, tile), :] = jnp.zeros((tile, LANES), F32)
    for at, copy in enumerate(copies):
        copy.wait()

        @pl.loop(0, piece // 16, unroll=4)
        def _(group):
            first = pl.multiple_of(at * piece + group * 16, 16)
            block = stage[pl.ds(first, 16), :].astype(F32)
            to = pl.multiple_of(first * chunks, 16)
            for h in range(2):
                for c in range(chunks):
                    rows[pl.ds(to + h * tile + c * SUBLANES, SUBLANES), :] = block[
                        h * SUBLANES : (h + 1) * SUBLANES, c * LANES : (c + 1) * LANES
                    ]

    @pl.loop(0, len(outs) * labels // SUBLANES)
    def _(group):
        for q in range(SUBLANES):
            first = (group * SUBLANES + q) * length
            terms = [
                rows[pl.ds(starts_ref[first + j], chunks, stride=SUBLANES), :] for j in range(length)
            ]
            while len(terms) > 1:
                terms = [a + b for a, b in zip(terms[::2], terms[1::2])] + terms[len(terms) // 2 * 2 :]
            sums[pl.ds(group * tile + q, chunks, stride=SUBLANES), :] = terms[0] / length

    for copy in moves:
        copy.wait()
    for n, out in enumerate(outs):
        for group in range(labels // 16):
            for c in range(chunks):
                at = ((n * labels) // SUBLANES + 2 * group) * tile + c * SUBLANES
                out[16 * group : 16 * group + 16, c * LANES : (c + 1) * LANES] = jnp.concatenate(
                    [sums[at : at + SUBLANES, :], sums[at + tile : at + tile + SUBLANES, :]]
                ).astype(out.dtype)


def block_kernel(docs_ref, positives_ref, owner_ref, row_ref, out):
    count, width = docs_ref.shape
    devices, labels = out.shape[0], owner_ref.shape[1]
    positives, row = positives_ref[...], row_ref[...]

    def spread(value):
        return jnp.broadcast_to(value.astype(F32).astype(BF16)[None], (devices,) + value.shape)

    out[:, :, width:] = jnp.zeros((devices, count, out.shape[2] - width), BF16)
    out[:, :, :width] = jnp.broadcast_to(docs_ref[...][None], (devices, count, width))
    for n in range(3):
        at = width + n * LANES
        out[:, :, at : at + positives.shape[1]] = spread((positives >> (8 * n)) & 255)
    at = width + 3 * LANES
    second = jnp.concatenate([row & 255] + [jnp.zeros_like(row)] * (count - 1))
    first = jnp.concatenate([owner_ref[...], second[:-1]])
    out[:, :, at : at + labels] = spread(first)
    out[:, :, at + labels : at + 2 * labels] = spread(
        jnp.concatenate([row >> 8] + [jnp.zeros_like(row)] * (count - 1))
    )


def docs_block(docs, positives, ref_owner, ref_row, devices):
    count, width = docs.shape
    labels = ref_row.shape[0]
    return pl.pallas_call(
        block_kernel,
        out_shape=jax.ShapeDtypeStruct((devices, count, width + 3 * LANES + 2 * labels), BF16),
        in_specs=[pl.BlockSpec(memory_space=pltpu.VMEM)] * 4,
        out_specs=pl.BlockSpec(memory_space=pltpu.VMEM),
    )(docs, positives, ref_owner.reshape(1, labels), ref_row.reshape(1, labels))


def partial_means(starts, near, far, after, labels, length, kinds, later=()):
    vocab_rows, width = near.shape
    chunks = width // LANES
    return pl.pallas_call(
        functools.partial(sum_kernel, length, 0 if after is None else 1 + len(later)),
        out_shape=[jax.ShapeDtypeStruct((labels, width), kind) for kind in kinds]
        + [jax.ShapeDtypeStruct(x.shape, x.dtype) for x in later]
        + [jax.ShapeDtypeStruct((SUBLANES, LANES), F32)],
        in_specs=[
            pl.BlockSpec(memory_space=pltpu.SMEM),
            pl.BlockSpec(memory_space=pl.ANY),
            pl.BlockSpec(memory_space=pl.ANY),
        ]
        + [pl.BlockSpec(memory_space=pltpu.VMEM)] * (after is not None)
        + [pl.BlockSpec(memory_space=pl.ANY) for _ in later],
        out_specs=[pl.BlockSpec(memory_space=pltpu.VMEM)] * (len(kinds) + len(later) + 1),
        scratch_shapes=[
            pltpu.VMEM((2 * vocab_rows, width), BF16),
            pltpu.VMEM(((2 * vocab_rows + 2 * SUBLANES) * chunks, LANES), F32),
            pltpu.VMEM(((len(kinds) * labels + SUBLANES) * chunks, LANES), F32),
            pltpu.SemaphoreType.DMA((2 * PIECES + len(later),)),
        ],
        compiler_params=pltpu.CompilerParams(vmem_limit_bytes=56 * 1024 * 1024),
        cost_estimate=pl.CostEstimate(
            flops=len(kinds) * labels * length * width,
            bytes_accessed=4 * vocab_rows * width,
            transcendentals=0,
        ),
    )(starts, near, far, *([] if after is None else [after]), *later)


def by_sums(
    token_table, enc_weight, enc_gain, label_tokens, ref_owner, ref_row, free_rows, docs, positives
):
    shards = lax.axis_size("shard")
    chips = shards // 2
    devices = shards * lax.axis_size("grp")
    me = lax.axis_index("shard")
    vocab_rows, width = token_table.shape
    labels, length = label_tokens.shape
    own_docs = docs.shape[0]
    all_count = devices * own_docs
    pos_count = positives.shape[1]
    slab_rows = free_rows.shape[0]
    tokens = labels * length
    label_cap = 2 * labels // shards
    others = [k for k in range(chips - 1, 0, -1)]

    other_table = swap_cores(token_table)

    asked = {k: to_chip(label_tokens, k) for k in others}
    asked[0] = label_tokens

    own_blocks = docs_block(docs, positives, ref_owner, ref_row, devices)
    own_blocks, asked[1] = lax.optimization_barrier((own_blocks, asked[1]))
    all_blocks = exchange(own_blocks, ALL)

    def starts(ks):
        ids = jnp.concatenate([asked[k] for k in ks])
        near = ids - me * vocab_rows
        far = ids - (me ^ 1) * vocab_rows
        row = jnp.where(
            (near >= 0) & (near < vocab_rows),
            near,
            jnp.where((far >= 0) & (far < vocab_rows), far + vocab_rows, 2 * vocab_rows),
        )
        first = (row // SUBLANES) * (SUBLANES * (width // LANES)) + row % SUBLANES
        return first.reshape(len(ks) * tokens)

    sent, after = [], None
    half = len(others) - len(others) // 3
    for ks in (others[:half], others[half:] + [0]):
        later = () if after is None else (free_rows,)
        *terms, note = partial_means(
            starts(ks), token_table, other_table, after, labels, length,
            [BF16 if k else F32 for k in ks], later
        )
        if later:
            *terms, free_rows = terms
        sent += terms
        after = swap_cores(note)
    arrived = [to_chip(term, k) for term, k in zip(sent, others)]
    all_blocks, pooled = lax.optimization_barrier((all_blocks, sent[-1]))
    all_docs = all_blocks[:, :, :width].reshape(all_count, width)
    low, middle, high = (
        all_blocks[:, :, at : at + pos_count].reshape(all_count, pos_count).astype(I32)
        for at in range(width, width + 3 * LANES, LANES)
    )
    all_positives = low + 256 * middle + 65536 * high

    info = lax.dynamic_slice_in_dim(all_blocks, lax.axis_index("grp") * shards, shards, 0)
    info = info[:, :, width + 3 * LANES :].astype(I32)
    owners = info[:, 0, :labels]
    rows = 256 * info[:, 0, labels:] + info[:, 1, :labels]
    marks = owners[:, None, :] == jnp.arange(shards, dtype=I32)[None, :, None]
    order = lax.broadcasted_iota(I32, (labels, labels), 0) < lax.broadcasted_iota(
        I32, (labels, labels), 1
    )
    before = jnp.dot(
        marks.reshape(shards * shards, labels).astype(BF16),
        order.astype(BF16),
        preferred_element_type=F32,
    ).reshape(shards, shards, labels)
    slot = jnp.sum(jnp.where(marks, before, 0.0), axis=1).astype(I32)
    slots = shards * label_cap
    source = jnp.arange(shards, dtype=I32)[:, None]
    coming = jnp.where(owners == me, (source ^ me) * label_cap + slot, -1).reshape(shards * labels)
    hit = jnp.arange(slots, dtype=I32)[:, None] == coming[None, :]
    got_rows = jnp.sum(jnp.where(hit, rows.reshape(shards * labels)[None, :] + 1, 0), axis=1) - 1
    going = jnp.where(
        (owners ^ me) % 2 == 0, ((owners ^ me) + (source ^ me) % 2) * label_cap + slot, -1
    )
    places = jnp.concatenate(
        [lax.dynamic_index_in_dim(going, me, 0, False), lax.dynamic_index_in_dim(going, me ^ 1, 0, False)]
    )
    to_slots = (jnp.arange(slots, dtype=I32)[:, None] == places[None, :]).astype(BF16)

    for term in arrived:
        pooled = pooled + term.astype(F32)
    pooled = pooled.astype(BF16)
    projected = jnp.dot(pooled, enc_weight, preferred_element_type=F32)
    norm_scale = lax.rsqrt(jnp.mean(projected * projected, axis=1, keepdims=True) + 1e-06)
    encoded = (projected * norm_scale * enc_gain * width ** (-0.5)).astype(BF16)

    both = jnp.concatenate([encoded, swap_cores(encoded)])
    send_vectors = jnp.dot(to_slots, both, preferred_element_type=F32).astype(BF16)
    send_vectors = send_vectors.reshape(chips, 2 * label_cap, width)
    arrived = {k: to_chip(send_vectors[k], k) for k in others}
    got_vectors = jnp.concatenate([send_vectors[0]] + [arrived[k] for k in range(1, chips)])
    to_rows = (jnp.arange(slab_rows, dtype=I32)[:, None] == got_rows[None, :]).astype(BF16)
    delta = jnp.dot(to_rows, got_vectors, preferred_element_type=F32)
    head = (free_rows.astype(F32) + delta).astype(BF16)

    label_columns = lax.axis_index(ALL) * slab_rows + jnp.arange(slab_rows, dtype=I32)
    logits = lax.dot_general(all_docs, head, (((1,), (1,)), ((), ())), preferred_element_type=F32)
    hits = jnp.zeros(logits.shape, jnp.bool_)
    for column in range(pos_count):
        hits = hits | (all_positives[:, column : column + 1] == label_columns[None, :])
    errors = (jax.nn.sigmoid(logits) - hits.astype(F32)).astype(BF16)
    doc_terms = jnp.dot(errors, head, preferred_element_type=F32)
    doc_terms = doc_terms.reshape(devices, own_docs, width)
    free_grad = lax.dot_general(
        errors, all_docs, (((0,), (0,)), ((), ())), preferred_element_type=F32
    ).astype(BF16)
    doc_terms, late_errors = lax.optimization_barrier((doc_terms, errors))
    doc_grad = jnp.sum(exchange(doc_terms, ALL), axis=0)
    picked = lax.dot_general(
        to_rows, late_errors, (((0,), (1,)), ((), ())), preferred_element_type=F32
    ).astype(BF16)
    picked = picked.reshape(chips, 2 * label_cap, all_count)
    arrived = {k: to_chip(picked[k], k) for k in others}
    returned = jnp.concatenate([picked[0]] + [arrived[k] for k in range(1, chips)])
    chip_errors = lax.dot_general(
        to_slots, returned, (((0,), (0,)), ((), ())), preferred_element_type=F32
    ).astype(BF16)
    ref_errors = chip_errors[:labels] + swap_cores(chip_errors[labels:])
    ref_grad = jnp.dot(ref_errors, all_docs, preferred_element_type=F32).astype(BF16)
    return (free_grad, doc_grad, ref_grad)


def on_device(token_table, enc_weight, enc_gain, label_tokens, *rest):
    shards = lax.axis_size("shard")
    labels, length = label_tokens.shape
    row_count = 5 * labels * length // 4
    plan = by_sums if shards % 2 == 0 and shards // 2 * labels < row_count else by_rows
    return plan(token_table, enc_weight, enc_gain, label_tokens, *rest)


def solution(mesh):
    in_specs = (
        P("shard", None),
        P(),
        P(),
        P(ALL, None),
        P(ALL, None),
        P(ALL),
        P(ALL, None),
        P(ALL, None),
        P(ALL, None),
    )
    out_specs = (P(ALL, None), P(ALL, None), P(ALL, None))
    return jax.shard_map(
        on_device, mesh=mesh, in_specs=in_specs, out_specs=out_specs, check_vma=False
    )
```

```python
import functools
import jax
import jax.numpy as jnp
from jax import lax
from jax.experimental import pallas as pl
from jax.experimental.pallas import tpu as pltpu
from jax.sharding import PartitionSpec as P

BF16 = jnp.bfloat16
F32 = jnp.float32
I32 = jnp.int32
ALL = ("grp", "shard")


def exchange(blocks, axes):
    return lax.all_to_all(blocks, axes, split_axis=0, concat_axis=0, tiled=True)


def inclusive_counts(marks):
    count = marks.shape[0]
    rows = lax.broadcasted_iota(I32, (count, count), 0)
    cols = lax.broadcasted_iota(I32, (count, count), 1)
    return jnp.dot((cols <= rows).astype(BF16), marks.astype(BF16), preferred_element_type=F32).astype(I32)


def token_places(owner, shards, cap):
    labels, length = owner.shape
    marks = (owner[:, :, None] == jnp.arange(shards, dtype=I32)).astype(I32)
    within = inclusive_counts(marks.reshape(labels, length * shards)).reshape(labels, length, shards)
    totals = within[-1]
    before = jnp.cumsum(totals, axis=0) - totals
    slot = jnp.sum((within + before[None] - 1) * marks, axis=2)
    return owner * cap + slot


def label_places(owner, shards, cap):
    marks = (owner[:, None] == jnp.arange(shards, dtype=I32)).astype(I32)
    slot = jnp.sum((inclusive_counts(marks) - 1) * marks, axis=1)
    return owner * cap + slot


def placed(values, places, size):
    hit = places[:, None] == jnp.arange(size, dtype=I32)[None, :]
    return jnp.sum(jnp.where(hit, values[:, None] + 1, 0), axis=0) - 1


def swap_cores(x):
    return lax.ppermute(x, "shard", [(i, i ^ 1) for i in range(lax.axis_size("shard"))])


def to_chip(x, k):
    return lax.ppermute(x, "shard", [(i, i ^ (2 * k)) for i in range(lax.axis_size("shard"))])


def by_rows(
    token_table, enc_weight, enc_gain, label_tokens, ref_owner, ref_row, free_rows, docs, positives
):
    shards = lax.axis_size("shard")
    devices = shards * lax.axis_size("grp")
    vocab_rows, width = token_table.shape
    labels, length = label_tokens.shape
    own_docs = docs.shape[0]
    pos_count = positives.shape[1]
    slab_rows = free_rows.shape[0]
    tokens = labels * length
    token_cap = 5 * tokens // (4 * shards)
    label_cap = 2 * labels // shards

    token_owner = label_tokens // vocab_rows
    token_dest = token_places(token_owner, shards, token_cap)
    send_ids = placed(
        (label_tokens - token_owner * vocab_rows).reshape(tokens),
        token_dest.reshape(tokens),
        shards * token_cap,
    )
    label_dest = label_places(ref_owner[:, 0], shards, label_cap)
    send_rows = placed(ref_row, label_dest, shards * label_cap)
    asked = exchange(
        jnp.concatenate(
            [send_ids.reshape(shards, token_cap), send_rows.reshape(shards, label_cap)], axis=1
        ),
        "shard",
    )
    got_rows = asked[:, token_cap:].reshape(shards * label_cap)

    digits = jnp.concatenate(
        [positives & 255, (positives >> 8) & 255, positives >> 16], axis=1
    ).astype(BF16)
    own_block = jnp.concatenate(
        [docs, digits, jnp.zeros((own_docs, 128 - 3 * pos_count), BF16)], axis=1
    )
    all_blocks = exchange(
        jnp.broadcast_to(own_block[None], (devices, own_docs, width + 128)), ALL
    ).reshape(devices * own_docs, width + 128)
    all_docs = all_blocks[:, :width]
    d = all_blocks[:, width : width + 3 * pos_count].astype(I32)
    all_positives = d[:, :pos_count] + 256 * d[:, pos_count : 2 * pos_count] + 65536 * d[:, 2 * pos_count :]

    found = token_table[jnp.maximum(asked[:, :token_cap], 0)]
    token_found = exchange(found, "shard").reshape(shards * token_cap, width)
    pick_tokens = jnp.zeros((labels, shards * token_cap), F32)
    for j in range(length):
        pick_tokens += (
            token_dest[:, j : j + 1] == jnp.arange(shards * token_cap, dtype=I32)[None, :]
        ).astype(F32)
    pooled = jnp.dot(
        (pick_tokens / length).astype(BF16), token_found, preferred_element_type=F32
    ).astype(BF16)
    projected = jnp.dot(pooled, enc_weight, preferred_element_type=F32)
    norm_scale = lax.rsqrt(jnp.mean(projected * projected, axis=1, keepdims=True) + 1e-06)
    encoded = (projected * norm_scale * enc_gain * width ** (-0.5)).astype(BF16)

    to_slots = (
        jnp.arange(shards * label_cap, dtype=I32)[:, None] == label_dest[None, :]
    ).astype(BF16)
    send_vectors = jnp.dot(to_slots, encoded, preferred_element_type=F32).astype(BF16)
    got_vectors = exchange(send_vectors.reshape(shards, label_cap, width), "shard").reshape(
        shards * label_cap, width
    )
    to_rows = (jnp.arange(slab_rows, dtype=I32)[:, None] == got_rows[None, :]).astype(BF16)
    delta = jnp.dot(to_rows, got_vectors, preferred_element_type=F32)
    head = (free_rows.astype(F32) + delta).astype(BF16)

    label_columns = lax.axis_index(ALL) * slab_rows + jnp.arange(slab_rows, dtype=I32)
    logits = lax.dot_general(all_docs, head, (((1,), (1,)), ((), ())), preferred_element_type=F32)
    hits = jnp.zeros(logits.shape, jnp.bool_)
    for column in range(pos_count):
        hits = hits | (all_positives[:, column : column + 1] == label_columns[None, :])
    errors = (jax.nn.sigmoid(logits) - hits.astype(F32)).astype(BF16)
    doc_terms = jnp.dot(errors, head, preferred_element_type=F32)
    free_grad = lax.dot_general(
        errors, all_docs, (((0,), (0,)), ((), ())), preferred_element_type=F32
    ).astype(BF16)
    picked = lax.dot_general(
        to_rows, errors, (((0,), (1,)), ((), ())), preferred_element_type=F32
    ).astype(BF16)
    returned = exchange(picked.reshape(shards, label_cap, devices * own_docs), "shard").reshape(
        shards * label_cap, devices * own_docs
    )
    ref_errors = lax.dot_general(
        to_slots, returned, (((0,), (0,)), ((), ())), preferred_element_type=F32
    ).astype(BF16)
    ref_grad = jnp.dot(ref_errors, all_docs, preferred_element_type=F32).astype(BF16)
    doc_grad = jnp.sum(exchange(doc_terms.reshape(devices, own_docs, width), ALL), axis=0)
    return (free_grad, doc_grad, ref_grad)


LANES = 128
SUBLANES = 8
PIECES = 4


def sum_kernel(length, held, starts_ref, near_ref, far_ref, *refs):
    moved = held - 1 if held else 0
    refs = refs[1:] if held else refs
    sources, refs, targets, note, (stage, rows, sums, sems) = (
        refs[:moved], refs[moved : -5 - moved], refs[len(refs) - 5 - moved : -5], refs[-5], refs[-4:]
    )
    outs = refs
    note[...] = jnp.zeros(note.shape, F32)
    moves = [
        pltpu.make_async_copy(a, b, sems.at[2 * PIECES + n])
        for n, (a, b) in enumerate(zip(sources, targets))
    ]
    vocab_rows, width = near_ref.shape
    chunks = width // LANES
    tile = SUBLANES * chunks
    labels = outs[0].shape[0]
    piece = vocab_rows // PIECES

    copies = []
    for half, table in enumerate((near_ref, far_ref)):
        for p in range(PIECES):
            at = half * PIECES + p
            copies.append(
                pltpu.make_async_copy(
                    table.at[pl.ds(p * piece, piece)], stage.at[pl.ds(at * piece, piece)], sems.at[at]
                )
            )
    for copy in copies + moves:
        copy.start()
    rows[pl.ds(2 * vocab_rows * chunks, tile), :] = jnp.zeros((tile, LANES), F32)
    for at, copy in enumerate(copies):
        copy.wait()

        @pl.loop(0, piece // 16, unroll=4)
        def _(group):
            first = pl.multiple_of(at * piece + group * 16, 16)
            block = stage[pl.ds(first, 16), :].astype(F32)
            to = pl.multiple_of(first * chunks, 16)
            for h in range(2):
                for c in range(chunks):
                    rows[pl.ds(to + h * tile + c * SUBLANES, SUBLANES), :] = block[
                        h * SUBLANES : (h + 1) * SUBLANES, c * LANES : (c + 1) * LANES
                    ]

    @pl.loop(0, len(outs) * labels // SUBLANES)
    def _(group):
        for q in range(SUBLANES):
            first = (group * SUBLANES + q) * length
            terms = [
                rows[pl.ds(starts_ref[first + j], chunks, stride=SUBLANES), :] for j in range(length)
            ]
            while len(terms) > 1:
                terms = [a + b for a, b in zip(terms[::2], terms[1::2])] + terms[len(terms) // 2 * 2 :]
            sums[pl.ds(group * tile + q, chunks, stride=SUBLANES), :] = terms[0] / length

    for copy in moves:
        copy.wait()
    for n, out in enumerate(outs):
        for group in range(labels // 16):
            for c in range(chunks):
                at = ((n * labels) // SUBLANES + 2 * group) * tile + c * SUBLANES
                out[16 * group : 16 * group + 16, c * LANES : (c + 1) * LANES] = jnp.concatenate(
                    [sums[at : at + SUBLANES, :], sums[at + tile : at + tile + SUBLANES, :]]
                ).astype(out.dtype)


def block_kernel(docs_ref, positives_ref, owner_ref, row_ref, out):
    count, width = docs_ref.shape
    devices, labels = out.shape[0], owner_ref.shape[1]
    positives, row = positives_ref[...], row_ref[...]

    def spread(value):
        return jnp.broadcast_to(value.astype(F32).astype(BF16)[None], (devices,) + value.shape)

    out[:, :, width:] = jnp.zeros((devices, count, out.shape[2] - width), BF16)
    out[:, :, :width] = jnp.broadcast_to(docs_ref[...][None], (devices, count, width))
    for n in range(3):
        at = width + n * LANES
        out[:, :, at : at + positives.shape[1]] = spread((positives >> (8 * n)) & 255)
    at = width + 3 * LANES
    second = jnp.concatenate([row & 255] + [jnp.zeros_like(row)] * (count - 1))
    first = jnp.concatenate([owner_ref[...], second[:-1]])
    out[:, :, at : at + labels] = spread(first)
    out[:, :, at + labels : at + 2 * labels] = spread(
        jnp.concatenate([row >> 8] + [jnp.zeros_like(row)] * (count - 1))
    )


def docs_block(docs, positives, ref_owner, ref_row, devices):
    count, width = docs.shape
    labels = ref_row.shape[0]
    return pl.pallas_call(
        block_kernel,
        out_shape=jax.ShapeDtypeStruct((devices, count, width + 3 * LANES + 2 * labels), BF16),
        in_specs=[pl.BlockSpec(memory_space=pltpu.VMEM)] * 4,
        out_specs=pl.BlockSpec(memory_space=pltpu.VMEM),
    )(docs, positives, ref_owner.reshape(1, labels), ref_row.reshape(1, labels))


def partial_means(starts, near, far, after, labels, length, kinds, later=()):
    vocab_rows, width = near.shape
    chunks = width // LANES
    return pl.pallas_call(
        functools.partial(sum_kernel, length, 0 if after is None else 1 + len(later)),
        out_shape=[jax.ShapeDtypeStruct((labels, width), kind) for kind in kinds]
        + [jax.ShapeDtypeStruct(x.shape, x.dtype) for x in later]
        + [jax.ShapeDtypeStruct((SUBLANES, LANES), F32)],
        in_specs=[
            pl.BlockSpec(memory_space=pltpu.SMEM),
            pl.BlockSpec(memory_space=pl.ANY),
            pl.BlockSpec(memory_space=pl.ANY),
        ]
        + [pl.BlockSpec(memory_space=pltpu.VMEM)] * (after is not None)
        + [pl.BlockSpec(memory_space=pl.ANY) for _ in later],
        out_specs=[pl.BlockSpec(memory_space=pltpu.VMEM)] * (len(kinds) + len(later) + 1),
        scratch_shapes=[
            pltpu.VMEM((2 * vocab_rows, width), BF16),
            pltpu.VMEM(((2 * vocab_rows + 2 * SUBLANES) * chunks, LANES), F32),
            pltpu.VMEM(((len(kinds) * labels + SUBLANES) * chunks, LANES), F32),
            pltpu.SemaphoreType.DMA((2 * PIECES + len(later),)),
        ],
        compiler_params=pltpu.CompilerParams(
            vmem_limit_bytes=(56 if after is None else 52) * 1024 * 1024
        ),
        cost_estimate=pl.CostEstimate(
            flops=len(kinds) * labels * length * width,
            bytes_accessed=4 * vocab_rows * width,
            transcendentals=0,
        ),
    )(starts, near, far, *([] if after is None else [after]), *later)


def by_sums(
    token_table, enc_weight, enc_gain, label_tokens, ref_owner, ref_row, free_rows, docs, positives
):
    shards = lax.axis_size("shard")
    chips = shards // 2
    devices = shards * lax.axis_size("grp")
    me = lax.axis_index("shard")
    vocab_rows, width = token_table.shape
    labels, length = label_tokens.shape
    own_docs = docs.shape[0]
    all_count = devices * own_docs
    pos_count = positives.shape[1]
    slab_rows = free_rows.shape[0]
    tokens = labels * length
    label_cap = 2 * labels // shards
    others = [k for k in range(chips - 1, 0, -1)]

    other_table = swap_cores(token_table)

    asked = {k: to_chip(label_tokens, k) for k in others}
    asked[0] = label_tokens

    own_blocks = docs_block(docs, positives, ref_owner, ref_row, devices)
    own_blocks, asked[1] = lax.optimization_barrier((own_blocks, asked[1]))
    all_blocks = exchange(own_blocks, ALL)

    def starts(ks):
        ids = jnp.concatenate([asked[k] for k in ks])
        near = ids - me * vocab_rows
        far = ids - (me ^ 1) * vocab_rows
        row = jnp.where(
            (near >= 0) & (near < vocab_rows),
            near,
            jnp.where((far >= 0) & (far < vocab_rows), far + vocab_rows, 2 * vocab_rows),
        )
        first = (row // SUBLANES) * (SUBLANES * (width // LANES)) + row % SUBLANES
        return first.reshape(len(ks) * tokens)

    sent, after = [], None
    half = len(others) - len(others) // 3
    for ks in (others[:half], others[half:] + [0]):
        later = () if after is None else (free_rows, enc_weight)
        *terms, note = partial_means(
            starts(ks), token_table, other_table, after, labels, length,
            [BF16 if k else F32 for k in ks], later
        )
        if later:
            *terms, free_rows, enc_weight = terms
        sent += terms
        after = swap_cores(note)
    arrived = [to_chip(term, k) for term, k in zip(sent, others)]
    all_blocks, pooled = lax.optimization_barrier((all_blocks, sent[-1]))
    all_docs = all_blocks[:, :, :width].reshape(all_count, width)
    low, middle, high = (
        all_blocks[:, :, at : at + pos_count].reshape(all_count, pos_count).astype(I32)
        for at in range(width, width + 3 * LANES, LANES)
    )
    all_positives = low + 256 * middle + 65536 * high

    info = lax.dynamic_slice_in_dim(all_blocks, lax.axis_index("grp") * shards, shards, 0)
    info = info[:, :, width + 3 * LANES :].astype(I32)
    owners = info[:, 0, :labels]
    rows = 256 * info[:, 0, labels:] + info[:, 1, :labels]
    marks = owners[:, None, :] == jnp.arange(shards, dtype=I32)[None, :, None]
    order = lax.broadcasted_iota(I32, (labels, labels), 0) < lax.broadcasted_iota(
        I32, (labels, labels), 1
    )
    before = jnp.dot(
        marks.reshape(shards * shards, labels).astype(BF16),
        order.astype(BF16),
        preferred_element_type=F32,
    ).reshape(shards, shards, labels)
    slot = jnp.sum(jnp.where(marks, before, 0.0), axis=1).astype(I32)
    slots = shards * label_cap
    source = jnp.arange(shards, dtype=I32)[:, None]
    coming = jnp.where(owners == me, (source ^ me) * label_cap + slot, -1).reshape(shards * labels)
    hit = jnp.arange(slots, dtype=I32)[:, None] == coming[None, :]
    got_rows = jnp.sum(jnp.where(hit, rows.reshape(shards * labels)[None, :] + 1, 0), axis=1) - 1
    going = jnp.where(
        (owners ^ me) % 2 == 0, ((owners ^ me) + (source ^ me) % 2) * label_cap + slot, -1
    )
    places = jnp.concatenate(
        [lax.dynamic_index_in_dim(going, me, 0, False), lax.dynamic_index_in_dim(going, me ^ 1, 0, False)]
    )
    to_slots = (jnp.arange(slots, dtype=I32)[:, None] == places[None, :]).astype(BF16)

    for term in arrived:
        pooled = pooled + term.astype(F32)
    pooled = pooled.astype(BF16)
    projected = jnp.dot(pooled, enc_weight, preferred_element_type=F32)
    norm_scale = lax.rsqrt(jnp.mean(projected * projected, axis=1, keepdims=True) + 1e-06)
    encoded = (projected * norm_scale * enc_gain * width ** (-0.5)).astype(BF16)

    both = jnp.concatenate([encoded, swap_cores(encoded)])
    send_vectors = jnp.dot(to_slots, both, preferred_element_type=F32).astype(BF16)
    send_vectors = send_vectors.reshape(chips, 2 * label_cap, width)
    arrived = {k: to_chip(send_vectors[k], k) for k in others}
    got_vectors = jnp.concatenate([send_vectors[0]] + [arrived[k] for k in range(1, chips)])
    to_rows = (jnp.arange(slab_rows, dtype=I32)[:, None] == got_rows[None, :]).astype(BF16)
    delta = jnp.dot(to_rows, got_vectors, preferred_element_type=F32)
    head = (free_rows.astype(F32) + delta).astype(BF16)

    label_columns = lax.axis_index(ALL) * slab_rows + jnp.arange(slab_rows, dtype=I32)
    logits = lax.dot_general(all_docs, head, (((1,), (1,)), ((), ())), preferred_element_type=F32)
    hits = jnp.zeros(logits.shape, jnp.bool_)
    for column in range(pos_count):
        hits = hits | (all_positives[:, column : column + 1] == label_columns[None, :])
    errors = (jax.nn.sigmoid(logits) - hits.astype(F32)).astype(BF16)
    doc_terms = jnp.dot(errors, head, preferred_element_type=F32)
    doc_terms = doc_terms.reshape(devices, own_docs, width)
    free_grad = lax.dot_general(
        errors, all_docs, (((0,), (0,)), ((), ())), preferred_element_type=F32
    ).astype(BF16)
    doc_terms, late_errors = lax.optimization_barrier((doc_terms, errors))
    doc_parts = exchange(doc_terms, ALL)
    picked = lax.dot_general(
        to_rows, late_errors, (((0,), (1,)), ((), ())), preferred_element_type=F32
    ).astype(BF16)
    picked = picked.reshape(chips, 2 * label_cap, all_count)
    arrived = {k: to_chip(picked[k], k) for k in others}
    returned = jnp.concatenate([picked[0]] + [arrived[k] for k in range(1, chips)])
    returned, doc_parts = lax.optimization_barrier((returned, doc_parts))
    doc_grad = jnp.sum(doc_parts, axis=0)
    chip_errors = lax.dot_general(
        to_slots, returned, (((0,), (0,)), ((), ())), preferred_element_type=F32
    ).astype(BF16)
    ref_errors = chip_errors[:labels] + swap_cores(chip_errors[labels:])
    ref_grad = jnp.dot(ref_errors, all_docs, preferred_element_type=F32).astype(BF16)
    return (free_grad, doc_grad, ref_grad)


def on_device(token_table, enc_weight, enc_gain, label_tokens, *rest):
    shards = lax.axis_size("shard")
    labels, length = label_tokens.shape
    row_count = 5 * labels * length // 4
    plan = by_sums if shards % 2 == 0 and shards // 2 * labels < row_count else by_rows
    return plan(token_table, enc_weight, enc_gain, label_tokens, *rest)


def solution(mesh):
    in_specs = (
        P("shard", None),
        P(),
        P(),
        P(ALL, None),
        P(ALL, None),
        P(ALL),
        P(ALL, None),
        P(ALL, None),
        P(ALL, None),
    )
    out_specs = (P(ALL, None), P(ALL, None), P(ALL, None))
    return jax.shard_map(
        on_device, mesh=mesh, in_specs=in_specs, out_specs=out_specs, check_vma=False
    )
```

```python
import functools
import jax
import jax.numpy as jnp
from jax import lax
from jax.experimental import pallas as pl
from jax.experimental.pallas import tpu as pltpu
from jax.sharding import PartitionSpec as P

BF16 = jnp.bfloat16
F32 = jnp.float32
I32 = jnp.int32
ALL = ("grp", "shard")


def exchange(blocks, axes):
    return lax.all_to_all(blocks, axes, split_axis=0, concat_axis=0, tiled=True)


def inclusive_counts(marks):
    count = marks.shape[0]
    rows = lax.broadcasted_iota(I32, (count, count), 0)
    cols = lax.broadcasted_iota(I32, (count, count), 1)
    return jnp.dot((cols <= rows).astype(BF16), marks.astype(BF16), preferred_element_type=F32).astype(I32)


def token_places(owner, shards, cap):
    labels, length = owner.shape
    marks = (owner[:, :, None] == jnp.arange(shards, dtype=I32)).astype(I32)
    within = inclusive_counts(marks.reshape(labels, length * shards)).reshape(labels, length, shards)
    totals = within[-1]
    before = jnp.cumsum(totals, axis=0) - totals
    slot = jnp.sum((within + before[None] - 1) * marks, axis=2)
    return owner * cap + slot


def label_places(owner, shards, cap):
    marks = (owner[:, None] == jnp.arange(shards, dtype=I32)).astype(I32)
    slot = jnp.sum((inclusive_counts(marks) - 1) * marks, axis=1)
    return owner * cap + slot


def placed(values, places, size):
    hit = places[:, None] == jnp.arange(size, dtype=I32)[None, :]
    return jnp.sum(jnp.where(hit, values[:, None] + 1, 0), axis=0) - 1


def swap_cores(x):
    return lax.ppermute(x, "shard", [(i, i ^ 1) for i in range(lax.axis_size("shard"))])


def to_chip(x, k):
    return lax.ppermute(x, "shard", [(i, i ^ (2 * k)) for i in range(lax.axis_size("shard"))])


def by_rows(
    token_table, enc_weight, enc_gain, label_tokens, ref_owner, ref_row, free_rows, docs, positives
):
    shards = lax.axis_size("shard")
    devices = shards * lax.axis_size("grp")
    vocab_rows, width = token_table.shape
    labels, length = label_tokens.shape
    own_docs = docs.shape[0]
    pos_count = positives.shape[1]
    slab_rows = free_rows.shape[0]
    tokens = labels * length
    token_cap = 5 * tokens // (4 * shards)
    label_cap = 2 * labels // shards

    token_owner = label_tokens // vocab_rows
    token_dest = token_places(token_owner, shards, token_cap)
    send_ids = placed(
        (label_tokens - token_owner * vocab_rows).reshape(tokens),
        token_dest.reshape(tokens),
        shards * token_cap,
    )
    label_dest = label_places(ref_owner[:, 0], shards, label_cap)
    send_rows = placed(ref_row, label_dest, shards * label_cap)
    asked = exchange(
        jnp.concatenate(
            [send_ids.reshape(shards, token_cap), send_rows.reshape(shards, label_cap)], axis=1
        ),
        "shard",
    )
    got_rows = asked[:, token_cap:].reshape(shards * label_cap)

    digits = jnp.concatenate(
        [positives & 255, (positives >> 8) & 255, positives >> 16], axis=1
    ).astype(BF16)
    own_block = jnp.concatenate(
        [docs, digits, jnp.zeros((own_docs, 128 - 3 * pos_count), BF16)], axis=1
    )
    all_blocks = exchange(
        jnp.broadcast_to(own_block[None], (devices, own_docs, width + 128)), ALL
    ).reshape(devices * own_docs, width + 128)
    all_docs = all_blocks[:, :width]
    d = all_blocks[:, width : width + 3 * pos_count].astype(I32)
    all_positives = d[:, :pos_count] + 256 * d[:, pos_count : 2 * pos_count] + 65536 * d[:, 2 * pos_count :]

    found = token_table[jnp.maximum(asked[:, :token_cap], 0)]
    token_found = exchange(found, "shard").reshape(shards * token_cap, width)
    pick_tokens = jnp.zeros((labels, shards * token_cap), F32)
    for j in range(length):
        pick_tokens += (
            token_dest[:, j : j + 1] == jnp.arange(shards * token_cap, dtype=I32)[None, :]
        ).astype(F32)
    pooled = jnp.dot(
        (pick_tokens / length).astype(BF16), token_found, preferred_element_type=F32
    ).astype(BF16)
    projected = jnp.dot(pooled, enc_weight, preferred_element_type=F32)
    norm_scale = lax.rsqrt(jnp.mean(projected * projected, axis=1, keepdims=True) + 1e-06)
    encoded = (projected * norm_scale * enc_gain * width ** (-0.5)).astype(BF16)

    to_slots = (
        jnp.arange(shards * label_cap, dtype=I32)[:, None] == label_dest[None, :]
    ).astype(BF16)
    send_vectors = jnp.dot(to_slots, encoded, preferred_element_type=F32).astype(BF16)
    got_vectors = exchange(send_vectors.reshape(shards, label_cap, width), "shard").reshape(
        shards * label_cap, width
    )
    to_rows = (jnp.arange(slab_rows, dtype=I32)[:, None] == got_rows[None, :]).astype(BF16)
    delta = jnp.dot(to_rows, got_vectors, preferred_element_type=F32)
    head = (free_rows.astype(F32) + delta).astype(BF16)

    label_columns = lax.axis_index(ALL) * slab_rows + jnp.arange(slab_rows, dtype=I32)
    logits = lax.dot_general(all_docs, head, (((1,), (1,)), ((), ())), preferred_element_type=F32)
    hits = jnp.zeros(logits.shape, jnp.bool_)
    for column in range(pos_count):
        hits = hits | (all_positives[:, column : column + 1] == label_columns[None, :])
    errors = (jax.nn.sigmoid(logits) - hits.astype(F32)).astype(BF16)
    doc_terms = jnp.dot(errors, head, preferred_element_type=F32)
    free_grad = lax.dot_general(
        errors, all_docs, (((0,), (0,)), ((), ())), preferred_element_type=F32
    ).astype(BF16)
    picked = lax.dot_general(
        to_rows, errors, (((0,), (1,)), ((), ())), preferred_element_type=F32
    ).astype(BF16)
    returned = exchange(picked.reshape(shards, label_cap, devices * own_docs), "shard").reshape(
        shards * label_cap, devices * own_docs
    )
    ref_errors = lax.dot_general(
        to_slots, returned, (((0,), (0,)), ((), ())), preferred_element_type=F32
    ).astype(BF16)
    ref_grad = jnp.dot(ref_errors, all_docs, preferred_element_type=F32).astype(BF16)
    doc_grad = jnp.sum(exchange(doc_terms.reshape(devices, own_docs, width), ALL), axis=0)
    return (free_grad, doc_grad, ref_grad)


LANES = 128
SUBLANES = 8
PIECES = 4


def sum_kernel(count, moved, held, me_ref, *refs):
    ids_refs, (near_ref, far_ref), refs = refs[:count], refs[count : count + 2], refs[count + 2 :]
    refs = refs[1:] if held else refs
    sources, outs, targets = refs[:moved], refs[moved : moved + count], refs[moved + count : -7]
    note, stage, rows, sums, found, starts, sems = refs[-7:]
    note[...] = jnp.zeros(note.shape, F32)
    moves = [
        pltpu.make_async_copy(a, b, sems.at[2 * PIECES + 1 + n])
        for n, (a, b) in enumerate(zip(sources, targets))
    ]
    vocab_rows, width = near_ref.shape
    length, labels = ids_refs[0].shape
    chunks = width // LANES
    tile = SUBLANES * chunks
    piece = vocab_rows // PIECES
    core = me_ref[0] & 1
    bases = (core * vocab_rows, (1 - core) * vocab_rows)

    copies = []
    for half, table in enumerate((near_ref, far_ref)):
        for p in range(PIECES):
            at = half * PIECES + p
            copies.append(
                pltpu.make_async_copy(
                    table.at[pl.ds(p * piece, piece)],
                    stage.at[pl.ds(pl.multiple_of(bases[half] + p * piece, 16), piece)],
                    sems.at[at],
                )
            )
    for copy in copies + moves:
        copy.start()
    for n, ids_ref in enumerate(ids_refs):
        row = ids_ref[...] - (me_ref[0] >> 1) * (2 * vocab_rows)
        row = jnp.where((row >= 0) & (row < 2 * vocab_rows), row, 2 * vocab_rows)
        found[n * length : (n + 1) * length, :] = (row >> 3) * tile + (row & 7)
    place = pltpu.make_async_copy(found, starts, sems.at[2 * PIECES])
    place.start()
    rows[pl.ds(2 * vocab_rows * chunks, tile), :] = jnp.zeros((tile, LANES), F32)
    for at, copy in enumerate(copies):
        copy.wait()

        @pl.loop(0, piece // 16, unroll=4)
        def _(group):
            first = pl.multiple_of(bases[at // PIECES] + at % PIECES * piece + group * 16, 16)
            block = stage[pl.ds(first, 16), :].astype(F32)
            to = pl.multiple_of(first * chunks, 16)
            for h in range(2):
                for c in range(chunks):
                    rows[pl.ds(to + h * tile + c * SUBLANES, SUBLANES), :] = block[
                        h * SUBLANES : (h + 1) * SUBLANES, c * LANES : (c + 1) * LANES
                    ]

    place.wait()
    for n in range(count):

        @pl.loop(0, labels // SUBLANES)
        def _(group):
            for q in range(SUBLANES):
                label = group * SUBLANES + q
                terms = [
                    rows[pl.ds(starts[n * length + j, label], chunks, stride=SUBLANES), :]
                    for j in range(length)
                ]
                while len(terms) > 1:
                    terms = [a + b for a, b in zip(terms[::2], terms[1::2])] + terms[len(terms) // 2 * 2 :]
                to = (n * labels // SUBLANES + group) * tile + q
                sums[pl.ds(to, chunks, stride=SUBLANES), :] = terms[0] / length

    for copy in moves:
        copy.wait()
    for n, out in enumerate(outs):
        for group in range(labels // 16):
            for c in range(chunks):
                at = ((n * labels) // SUBLANES + 2 * group) * tile + c * SUBLANES
                out[16 * group : 16 * group + 16, c * LANES : (c + 1) * LANES] = jnp.concatenate(
                    [sums[at : at + SUBLANES, :], sums[at + tile : at + tile + SUBLANES, :]]
                ).astype(out.dtype)


def block_kernel(docs_ref, positives_ref, owner_ref, row_ref, out):
    count, width = docs_ref.shape
    devices, labels = out.shape[0], owner_ref.shape[1]
    positives, row = positives_ref[...], row_ref[...]

    def spread(value):
        return jnp.broadcast_to(value.astype(F32).astype(BF16)[None], (devices,) + value.shape)

    out[:, :, width:] = jnp.zeros((devices, count, out.shape[2] - width), BF16)
    out[:, :, :width] = jnp.broadcast_to(docs_ref[...][None], (devices, count, width))
    for n in range(3):
        at = width + n * LANES
        out[:, :, at : at + positives.shape[1]] = spread((positives >> (8 * n)) & 255)
    at = width + 3 * LANES
    second = jnp.concatenate([row & 255] + [jnp.zeros_like(row)] * (count - 1))
    first = jnp.concatenate([owner_ref[...], second[:-1]])
    out[:, :, at : at + labels] = spread(first)
    out[:, :, at + labels : at + 2 * labels] = spread(
        jnp.concatenate([row >> 8] + [jnp.zeros_like(row)] * (count - 1))
    )


def docs_block(docs, positives, ref_owner, ref_row, devices):
    count, width = docs.shape
    labels = ref_row.shape[0]
    return pl.pallas_call(
        block_kernel,
        out_shape=jax.ShapeDtypeStruct((devices, count, width + 3 * LANES + 2 * labels), BF16),
        in_specs=[pl.BlockSpec(memory_space=pltpu.VMEM)] * 4,
        out_specs=pl.BlockSpec(memory_space=pltpu.VMEM),
    )(docs, positives, ref_owner.reshape(1, labels), ref_row.reshape(1, labels))


def partial_means(me, ids, near, far, after, kinds, later=()):
    vocab_rows, width = near.shape
    chunks = width // LANES
    length, labels = ids[0].shape
    held = [] if after is None else [after]
    return pl.pallas_call(
        functools.partial(sum_kernel, len(kinds), len(later), bool(held)),
        out_shape=[jax.ShapeDtypeStruct((labels, width), kind) for kind in kinds]
        + [jax.ShapeDtypeStruct(x.shape, x.dtype) for x in later]
        + [jax.ShapeDtypeStruct((SUBLANES, LANES), F32)],
        in_specs=[pl.BlockSpec(memory_space=pltpu.SMEM)]
        + [pl.BlockSpec(memory_space=pltpu.VMEM)] * len(ids)
        + [pl.BlockSpec(memory_space=pl.ANY)] * 2
        + [pl.BlockSpec(memory_space=pltpu.VMEM) for _ in held]
        + [pl.BlockSpec(memory_space=pl.ANY) for _ in later],
        out_specs=[pl.BlockSpec(memory_space=pltpu.VMEM)] * (len(kinds) + len(later) + 1),
        scratch_shapes=[
            pltpu.VMEM((2 * vocab_rows, width), BF16),
            pltpu.VMEM(((2 * vocab_rows + 2 * SUBLANES) * chunks, LANES), F32),
            pltpu.VMEM(((len(kinds) * labels + SUBLANES) * chunks, LANES), F32),
            pltpu.VMEM((len(ids) * length, labels), I32),
            pltpu.SMEM((len(ids) * length, labels), I32),
            pltpu.SemaphoreType.DMA((2 * PIECES + 1 + len(later),)),
        ],
        compiler_params=pltpu.CompilerParams(
            vmem_limit_bytes=(56 if after is None else 52) * 1024 * 1024
        ),
        cost_estimate=pl.CostEstimate(
            flops=len(kinds) * labels * length * width,
            bytes_accessed=4 * vocab_rows * width,
            transcendentals=0,
        ),
    )(me, *ids, near, far, *held, *later)


def grad_kernel(errors_ref, docs_ref, out_ref):
    out_ref[...] = lax.dot_general(
        errors_ref[...], docs_ref[...], (((0,), (0,)), ((), ())), preferred_element_type=F32
    ).astype(BF16)


def rows_grad(errors, docs):
    count, slab_rows = errors.shape
    width = docs.shape[1]
    step = 256 if slab_rows % 256 == 0 else slab_rows
    return pl.pallas_call(
        grad_kernel,
        grid=(slab_rows // step,),
        out_shape=jax.ShapeDtypeStruct((slab_rows, width), BF16),
        in_specs=[
            pl.BlockSpec((count, step), lambda i: (0, i)),
            pl.BlockSpec((count, width), lambda i: (0, 0)),
        ],
        out_specs=pl.BlockSpec((step, width), lambda i: (i, 0)),
        compiler_params=pltpu.CompilerParams(vmem_limit_bytes=16 * 1024 * 1024),
        cost_estimate=pl.CostEstimate(flops=1, bytes_accessed=1, transcendentals=0),
    )(errors, docs)


def by_sums(
    token_table, enc_weight, enc_gain, label_tokens, ref_owner, ref_row, free_rows, docs, positives
):
    shards = lax.axis_size("shard")
    chips = shards // 2
    devices = shards * lax.axis_size("grp")
    me = lax.axis_index("shard")
    vocab_rows, width = token_table.shape
    labels, length = label_tokens.shape
    own_docs = docs.shape[0]
    all_count = devices * own_docs
    pos_count = positives.shape[1]
    slab_rows = free_rows.shape[0]
    tokens = labels * length
    label_cap = 2 * labels // shards
    others = [k for k in range(chips - 1, 0, -1)]

    other_table = swap_cores(token_table)

    ids = label_tokens.T
    asked = {k: to_chip(ids, k) for k in others}
    asked[0] = ids

    own_blocks = docs_block(docs, positives, ref_owner, ref_row, devices)
    own_blocks, asked = lax.optimization_barrier((own_blocks, asked))
    all_blocks = exchange(own_blocks, ALL)

    sent, after = [], None
    half = len(others) - len(others) // 3
    for ks in (others[:half], others[half:] + [0]):
        later = () if after is None else (free_rows, enc_weight)
        *terms, note = partial_means(
            me.reshape(1), [asked[k] for k in ks], token_table, other_table, after,
            [BF16 if k else F32 for k in ks], later
        )
        if later:
            *terms, free_rows, enc_weight = terms
        sent += terms
        after = swap_cores(note)
    arrived = [to_chip(term, k) for term, k in zip(sent, others)]
    all_blocks, pooled = lax.optimization_barrier((all_blocks, sent[-1]))
    all_docs = all_blocks[:, :, :width].reshape(all_count, width)
    low, middle, high = (
        all_blocks[:, :, at : at + pos_count].reshape(all_count, pos_count).astype(I32)
        for at in range(width, width + 3 * LANES, LANES)
    )
    all_positives = low + 256 * middle + 65536 * high

    info = lax.dynamic_slice_in_dim(all_blocks, lax.axis_index("grp") * shards, shards, 0)
    info = info[:, :, width + 3 * LANES :].astype(I32)
    owners = info[:, 0, :labels]
    rows = 256 * info[:, 0, labels:] + info[:, 1, :labels]
    marks = owners[:, None, :] == jnp.arange(shards, dtype=I32)[None, :, None]
    order = lax.broadcasted_iota(I32, (labels, labels), 0) < lax.broadcasted_iota(
        I32, (labels, labels), 1
    )
    before = jnp.dot(
        marks.reshape(shards * shards, labels).astype(BF16),
        order.astype(BF16),
        preferred_element_type=F32,
    ).reshape(shards, shards, labels)
    slot = jnp.sum(jnp.where(marks, before, 0.0), axis=1).astype(I32)
    slots = shards * label_cap
    source = jnp.arange(shards, dtype=I32)[:, None]
    coming = jnp.where(owners == me, (source ^ me) * label_cap + slot, -1).reshape(shards * labels)
    hit = jnp.arange(slots, dtype=I32)[:, None] == coming[None, :]
    got_rows = jnp.sum(jnp.where(hit, rows.reshape(shards * labels)[None, :] + 1, 0), axis=1) - 1
    going = jnp.where(
        (owners ^ me) % 2 == 0, ((owners ^ me) + (source ^ me) % 2) * label_cap + slot, -1
    )
    places = jnp.concatenate(
        [lax.dynamic_index_in_dim(going, me, 0, False), lax.dynamic_index_in_dim(going, me ^ 1, 0, False)]
    )
    to_slots = (jnp.arange(slots, dtype=I32)[:, None] == places[None, :]).astype(BF16)

    for term in arrived:
        pooled = pooled + term.astype(F32)
    pooled = pooled.astype(BF16)
    projected = jnp.dot(pooled, enc_weight, preferred_element_type=F32)
    norm_scale = lax.rsqrt(jnp.mean(projected * projected, axis=1, keepdims=True) + 1e-06)
    encoded = (projected * norm_scale * enc_gain * width ** (-0.5)).astype(BF16)

    both = jnp.concatenate([encoded, swap_cores(encoded)])
    send_vectors = jnp.dot(to_slots, both, preferred_element_type=F32).astype(BF16)
    send_vectors = send_vectors.reshape(chips, 2 * label_cap, width)
    arrived = {k: to_chip(send_vectors[k], k) for k in others}
    got_vectors = jnp.concatenate([send_vectors[0]] + [arrived[k] for k in range(1, chips)])
    to_rows = (jnp.arange(slab_rows, dtype=I32)[:, None] == got_rows[None, :]).astype(BF16)
    delta = jnp.dot(to_rows, got_vectors, preferred_element_type=F32)
    head = (free_rows.astype(F32) + delta).astype(BF16)

    label_columns = lax.axis_index(ALL) * slab_rows + jnp.arange(slab_rows, dtype=I32)
    logits = lax.dot_general(all_docs, head, (((1,), (1,)), ((), ())), preferred_element_type=F32)
    hits = jnp.zeros(logits.shape, jnp.bool_)
    for column in range(pos_count):
        hits = hits | (all_positives[:, column : column + 1] == label_columns[None, :])
    errors = (jax.nn.sigmoid(logits) - hits.astype(F32)).astype(BF16)
    doc_terms = jnp.dot(errors, head, preferred_element_type=F32)
    doc_terms = doc_terms.reshape(devices, own_docs, width)
    doc_terms, late_errors = lax.optimization_barrier((doc_terms, errors))
    doc_parts = exchange(doc_terms, ALL)
    picked = lax.dot_general(
        to_rows, late_errors, (((0,), (1,)), ((), ())), preferred_element_type=F32
    ).astype(BF16)
    picked = picked.reshape(chips, 2 * label_cap, all_count)
    arrived = {k: to_chip(picked[k], k) for k in others}
    returned = jnp.concatenate([picked[0]] + [arrived[k] for k in range(1, chips)])
    free_grad = rows_grad(errors, all_docs)
    returned, doc_parts, free_grad = lax.optimization_barrier((returned, doc_parts, free_grad))
    doc_grad = jnp.sum(doc_parts, axis=0)
    chip_errors = lax.dot_general(
        to_slots, returned, (((0,), (0,)), ((), ())), preferred_element_type=F32
    ).astype(BF16)
    ref_errors = chip_errors[:labels] + swap_cores(chip_errors[labels:])
    ref_grad = jnp.dot(ref_errors, all_docs, preferred_element_type=F32).astype(BF16)
    return (free_grad, doc_grad, ref_grad)


def on_device(token_table, enc_weight, enc_gain, label_tokens, *rest):
    shards = lax.axis_size("shard")
    labels, length = label_tokens.shape
    row_count = 5 * labels * length // 4
    plan = by_sums if shards % 2 == 0 and shards // 2 * labels < row_count else by_rows
    return plan(token_table, enc_weight, enc_gain, label_tokens, *rest)


def solution(mesh):
    in_specs = (
        P("shard", None),
        P(),
        P(),
        P(ALL, None),
        P(ALL, None),
        P(ALL),
        P(ALL, None),
        P(ALL, None),
        P(ALL, None),
    )
    out_specs = (P(ALL, None), P(ALL, None), P(ALL, None))
    return jax.shard_map(
        on_device, mesh=mesh, in_specs=in_specs, out_specs=out_specs, check_vma=False
    )
```

```python
import functools
import jax
import jax.numpy as jnp
from jax import lax
from jax.experimental import pallas as pl
from jax.experimental.pallas import tpu as pltpu
from jax.sharding import PartitionSpec as P

BF16 = jnp.bfloat16
F32 = jnp.float32
I32 = jnp.int32
ALL = ("grp", "shard")


def exchange(blocks, axes):
    return lax.all_to_all(blocks, axes, split_axis=0, concat_axis=0, tiled=True)


def inclusive_counts(marks):
    count = marks.shape[0]
    rows = lax.broadcasted_iota(I32, (count, count), 0)
    cols = lax.broadcasted_iota(I32, (count, count), 1)
    return jnp.dot((cols <= rows).astype(BF16), marks.astype(BF16), preferred_element_type=F32).astype(I32)


def token_places(owner, shards, cap):
    labels, length = owner.shape
    marks = (owner[:, :, None] == jnp.arange(shards, dtype=I32)).astype(I32)
    within = inclusive_counts(marks.reshape(labels, length * shards)).reshape(labels, length, shards)
    totals = within[-1]
    before = jnp.cumsum(totals, axis=0) - totals
    slot = jnp.sum((within + before[None] - 1) * marks, axis=2)
    return owner * cap + slot


def label_places(owner, shards, cap):
    marks = (owner[:, None] == jnp.arange(shards, dtype=I32)).astype(I32)
    slot = jnp.sum((inclusive_counts(marks) - 1) * marks, axis=1)
    return owner * cap + slot


def placed(values, places, size):
    hit = places[:, None] == jnp.arange(size, dtype=I32)[None, :]
    return jnp.sum(jnp.where(hit, values[:, None] + 1, 0), axis=0) - 1


def swap_cores(x):
    return lax.ppermute(x, "shard", [(i, i ^ 1) for i in range(lax.axis_size("shard"))])


def to_chip(x, k):
    return lax.ppermute(x, "shard", [(i, i ^ (2 * k)) for i in range(lax.axis_size("shard"))])


def by_rows(
    token_table, enc_weight, enc_gain, label_tokens, ref_owner, ref_row, free_rows, docs, positives
):
    shards = lax.axis_size("shard")
    devices = shards * lax.axis_size("grp")
    vocab_rows, width = token_table.shape
    labels, length = label_tokens.shape
    own_docs = docs.shape[0]
    pos_count = positives.shape[1]
    slab_rows = free_rows.shape[0]
    tokens = labels * length
    token_cap = 5 * tokens // (4 * shards)
    label_cap = 2 * labels // shards

    token_owner = label_tokens // vocab_rows
    token_dest = token_places(token_owner, shards, token_cap)
    send_ids = placed(
        (label_tokens - token_owner * vocab_rows).reshape(tokens),
        token_dest.reshape(tokens),
        shards * token_cap,
    )
    label_dest = label_places(ref_owner[:, 0], shards, label_cap)
    send_rows = placed(ref_row, label_dest, shards * label_cap)
    asked = exchange(
        jnp.concatenate(
            [send_ids.reshape(shards, token_cap), send_rows.reshape(shards, label_cap)], axis=1
        ),
        "shard",
    )
    got_rows = asked[:, token_cap:].reshape(shards * label_cap)

    digits = jnp.concatenate(
        [positives & 255, (positives >> 8) & 255, positives >> 16], axis=1
    ).astype(BF16)
    own_block = jnp.concatenate(
        [docs, digits, jnp.zeros((own_docs, 128 - 3 * pos_count), BF16)], axis=1
    )
    all_blocks = exchange(
        jnp.broadcast_to(own_block[None], (devices, own_docs, width + 128)), ALL
    ).reshape(devices * own_docs, width + 128)
    all_docs = all_blocks[:, :width]
    d = all_blocks[:, width : width + 3 * pos_count].astype(I32)
    all_positives = d[:, :pos_count] + 256 * d[:, pos_count : 2 * pos_count] + 65536 * d[:, 2 * pos_count :]

    found = token_table[jnp.maximum(asked[:, :token_cap], 0)]
    token_found = exchange(found, "shard").reshape(shards * token_cap, width)
    pick_tokens = jnp.zeros((labels, shards * token_cap), F32)
    for j in range(length):
        pick_tokens += (
            token_dest[:, j : j + 1] == jnp.arange(shards * token_cap, dtype=I32)[None, :]
        ).astype(F32)
    pooled = jnp.dot(
        (pick_tokens / length).astype(BF16), token_found, preferred_element_type=F32
    ).astype(BF16)
    projected = jnp.dot(pooled, enc_weight, preferred_element_type=F32)
    norm_scale = lax.rsqrt(jnp.mean(projected * projected, axis=1, keepdims=True) + 1e-06)
    encoded = (projected * norm_scale * enc_gain * width ** (-0.5)).astype(BF16)

    to_slots = (
        jnp.arange(shards * label_cap, dtype=I32)[:, None] == label_dest[None, :]
    ).astype(BF16)
    send_vectors = jnp.dot(to_slots, encoded, preferred_element_type=F32).astype(BF16)
    got_vectors = exchange(send_vectors.reshape(shards, label_cap, width), "shard").reshape(
        shards * label_cap, width
    )
    to_rows = (jnp.arange(slab_rows, dtype=I32)[:, None] == got_rows[None, :]).astype(BF16)
    delta = jnp.dot(to_rows, got_vectors, preferred_element_type=F32)
    head = (free_rows.astype(F32) + delta).astype(BF16)

    label_columns = lax.axis_index(ALL) * slab_rows + jnp.arange(slab_rows, dtype=I32)
    logits = lax.dot_general(all_docs, head, (((1,), (1,)), ((), ())), preferred_element_type=F32)
    hits = jnp.zeros(logits.shape, jnp.bool_)
    for column in range(pos_count):
        hits = hits | (all_positives[:, column : column + 1] == label_columns[None, :])
    errors = (jax.nn.sigmoid(logits) - hits.astype(F32)).astype(BF16)
    doc_terms = jnp.dot(errors, head, preferred_element_type=F32)
    free_grad = lax.dot_general(
        errors, all_docs, (((0,), (0,)), ((), ())), preferred_element_type=F32
    ).astype(BF16)
    picked = lax.dot_general(
        to_rows, errors, (((0,), (1,)), ((), ())), preferred_element_type=F32
    ).astype(BF16)
    returned = exchange(picked.reshape(shards, label_cap, devices * own_docs), "shard").reshape(
        shards * label_cap, devices * own_docs
    )
    ref_errors = lax.dot_general(
        to_slots, returned, (((0,), (0,)), ((), ())), preferred_element_type=F32
    ).astype(BF16)
    ref_grad = jnp.dot(ref_errors, all_docs, preferred_element_type=F32).astype(BF16)
    doc_grad = jnp.sum(exchange(doc_terms.reshape(devices, own_docs, width), ALL), axis=0)
    return (free_grad, doc_grad, ref_grad)


LANES = 128
SUBLANES = 8
PIECES = 8


def sum_kernel(count, moved, held, me_ref, *refs):
    ids_refs, (near_ref, far_ref), refs = refs[:count], refs[count : count + 2], refs[count + 2 :]
    refs = refs[1:] if held else refs
    sources, outs, targets = refs[:moved], refs[moved : moved + count], refs[moved + count : -7]
    note, stage, rows, sums, found, starts, sems = refs[-7:]
    note[...] = jnp.zeros(note.shape, F32)
    moves = [
        pltpu.make_async_copy(a, b, sems.at[2 * PIECES + 1 + n])
        for n, (a, b) in enumerate(zip(sources, targets))
    ]
    vocab_rows, width = near_ref.shape
    length, labels = ids_refs[0].shape
    chunks = width // LANES
    tile = SUBLANES * chunks
    piece = vocab_rows // PIECES
    core = me_ref[0] & 1
    bases = (core * vocab_rows, (1 - core) * vocab_rows)

    copies = []
    for half, table in enumerate((near_ref, far_ref)):
        for p in range(PIECES):
            at = half * PIECES + p
            copies.append(
                pltpu.make_async_copy(
                    table.at[pl.ds(p * piece, piece)],
                    stage.at[pl.ds(pl.multiple_of(bases[half] + p * piece, 16), piece)],
                    sems.at[at],
                )
            )
    for copy in copies + moves:
        copy.start()
    for n, ids_ref in enumerate(ids_refs):
        row = ids_ref[...] - (me_ref[0] >> 1) * (2 * vocab_rows)
        row = jnp.where((row >= 0) & (row < 2 * vocab_rows), row, 2 * vocab_rows)
        found[n * length : (n + 1) * length, :] = (row >> 3) * tile + (row & 7)
    place = pltpu.make_async_copy(found, starts, sems.at[2 * PIECES])
    place.start()
    rows[pl.ds(2 * vocab_rows * chunks, tile), :] = jnp.zeros((tile, LANES), F32)
    for at, copy in enumerate(copies):
        copy.wait()

        @pl.loop(0, piece // 16, unroll=6)
        def _(group):
            first = pl.multiple_of(bases[at // PIECES] + at % PIECES * piece + group * 16, 16)
            block = stage[pl.ds(first, 16), :].astype(F32)
            to = pl.multiple_of(first * chunks, 16)
            for h in range(2):
                for c in range(chunks):
                    rows[pl.ds(to + h * tile + c * SUBLANES, SUBLANES), :] = block[
                        h * SUBLANES : (h + 1) * SUBLANES, c * LANES : (c + 1) * LANES
                    ]

    place.wait()
    for n in range(count):

        @pl.loop(0, labels // SUBLANES, unroll=4)
        def _(group):
            for q in range(SUBLANES):
                label = group * SUBLANES + q
                terms = [
                    rows[pl.ds(starts[n * length + j, label], chunks, stride=SUBLANES), :]
                    for j in range(length)
                ]
                while len(terms) > 1:
                    terms = [a + b for a, b in zip(terms[::2], terms[1::2])] + terms[len(terms) // 2 * 2 :]
                to = (n * labels // SUBLANES + group) * tile + q
                sums[pl.ds(to, chunks, stride=SUBLANES), :] = terms[0] / length

    for copy in moves:
        copy.wait()
    for n, out in enumerate(outs):
        for group in range(labels // 16):
            for c in range(chunks):
                at = ((n * labels) // SUBLANES + 2 * group) * tile + c * SUBLANES
                out[16 * group : 16 * group + 16, c * LANES : (c + 1) * LANES] = jnp.concatenate(
                    [sums[at : at + SUBLANES, :], sums[at + tile : at + tile + SUBLANES, :]]
                ).astype(out.dtype)


def block_kernel(docs_ref, positives_ref, owner_ref, row_ref, out):
    count, width = docs_ref.shape
    devices, labels = out.shape[0], owner_ref.shape[1]
    positives, row = positives_ref[...], row_ref[...]

    def spread(value):
        return jnp.broadcast_to(value.astype(F32).astype(BF16)[None], (devices,) + value.shape)

    out[:, :, width:] = jnp.zeros((devices, count, out.shape[2] - width), BF16)
    out[:, :, :width] = jnp.broadcast_to(docs_ref[...][None], (devices, count, width))
    for n in range(3):
        at = width + n * LANES
        out[:, :, at : at + positives.shape[1]] = spread((positives >> (8 * n)) & 255)
    at = width + 3 * LANES
    second = jnp.concatenate([row & 255] + [jnp.zeros_like(row)] * (count - 1))
    first = jnp.concatenate([owner_ref[...], second[:-1]])
    out[:, :, at : at + labels] = spread(first)
    out[:, :, at + labels : at + 2 * labels] = spread(
        jnp.concatenate([row >> 8] + [jnp.zeros_like(row)] * (count - 1))
    )


def docs_block(docs, positives, ref_owner, ref_row, devices):
    count, width = docs.shape
    labels = ref_row.shape[0]
    return pl.pallas_call(
        block_kernel,
        out_shape=jax.ShapeDtypeStruct((devices, count, width + 3 * LANES + 2 * labels), BF16),
        in_specs=[pl.BlockSpec(memory_space=pltpu.VMEM)] * 4,
        out_specs=pl.BlockSpec(memory_space=pltpu.VMEM),
    )(docs, positives, ref_owner.reshape(1, labels), ref_row.reshape(1, labels))


def partial_means(me, ids, near, far, after, kinds, later=()):
    vocab_rows, width = near.shape
    chunks = width // LANES
    length, labels = ids[0].shape
    held = [] if after is None else [after]
    return pl.pallas_call(
        functools.partial(sum_kernel, len(kinds), len(later), bool(held)),
        out_shape=[jax.ShapeDtypeStruct((labels, width), kind) for kind in kinds]
        + [jax.ShapeDtypeStruct(x.shape, x.dtype) for x in later]
        + [jax.ShapeDtypeStruct((SUBLANES, LANES), F32)],
        in_specs=[pl.BlockSpec(memory_space=pltpu.SMEM)]
        + [pl.BlockSpec(memory_space=pltpu.VMEM)] * len(ids)
        + [pl.BlockSpec(memory_space=pl.ANY)] * 2
        + [pl.BlockSpec(memory_space=pltpu.VMEM) for _ in held]
        + [pl.BlockSpec(memory_space=pl.ANY) for _ in later],
        out_specs=[pl.BlockSpec(memory_space=pltpu.VMEM)] * (len(kinds) + len(later) + 1),
        scratch_shapes=[
            pltpu.VMEM((2 * vocab_rows, width), BF16),
            pltpu.VMEM(((2 * vocab_rows + 2 * SUBLANES) * chunks, LANES), F32),
            pltpu.VMEM(((len(kinds) * labels + SUBLANES) * chunks, LANES), F32),
            pltpu.VMEM((len(ids) * length, labels), I32),
            pltpu.SMEM((len(ids) * length, labels), I32),
            pltpu.SemaphoreType.DMA((2 * PIECES + 1 + len(later),)),
        ],
        compiler_params=pltpu.CompilerParams(
            vmem_limit_bytes=(56 if after is None else 52) * 1024 * 1024
        ),
        cost_estimate=pl.CostEstimate(
            flops=len(kinds) * labels * length * width,
            bytes_accessed=4 * vocab_rows * width,
            transcendentals=0,
        ),
    )(me, *ids, near, far, *held, *later)


def grad_kernel(errors_ref, docs_ref, out_ref):
    out_ref[...] = lax.dot_general(
        errors_ref[...], docs_ref[...], (((0,), (0,)), ((), ())), preferred_element_type=F32
    ).astype(BF16)


def rows_grad(errors, docs):
    count, slab_rows = errors.shape
    width = docs.shape[1]
    step = 256 if slab_rows % 256 == 0 else slab_rows
    return pl.pallas_call(
        grad_kernel,
        grid=(slab_rows // step,),
        out_shape=jax.ShapeDtypeStruct((slab_rows, width), BF16),
        in_specs=[
            pl.BlockSpec((count, step), lambda i: (0, i)),
            pl.BlockSpec((count, width), lambda i: (0, 0)),
        ],
        out_specs=pl.BlockSpec((step, width), lambda i: (i, 0)),
        compiler_params=pltpu.CompilerParams(vmem_limit_bytes=16 * 1024 * 1024),
        cost_estimate=pl.CostEstimate(flops=1, bytes_accessed=1, transcendentals=0),
    )(errors, docs)


def by_sums(
    token_table, enc_weight, enc_gain, label_tokens, ref_owner, ref_row, free_rows, docs, positives
):
    shards = lax.axis_size("shard")
    chips = shards // 2
    devices = shards * lax.axis_size("grp")
    me = lax.axis_index("shard")
    vocab_rows, width = token_table.shape
    labels, length = label_tokens.shape
    own_docs = docs.shape[0]
    all_count = devices * own_docs
    pos_count = positives.shape[1]
    slab_rows = free_rows.shape[0]
    tokens = labels * length
    label_cap = 2 * labels // shards
    others = [k for k in range(chips - 1, 0, -1)]

    other_table = swap_cores(token_table)

    ids = label_tokens.T
    asked = {k: to_chip(ids, k) for k in others}
    asked[0] = ids

    own_blocks = docs_block(docs, positives, ref_owner, ref_row, devices)
    own_blocks, asked = lax.optimization_barrier((own_blocks, asked))
    all_blocks = exchange(own_blocks, ALL)

    sent, after = [], None
    half = len(others) - len(others) // 3
    for ks in (others[:half], others[half:] + [0]):
        later = () if after is None else (free_rows, enc_weight)
        *terms, note = partial_means(
            me.reshape(1), [asked[k] for k in ks], token_table, other_table, after,
            [BF16 if k else F32 for k in ks], later
        )
        if later:
            *terms, free_rows, enc_weight = terms
        sent += terms
        after = swap_cores(note)
    arrived = [to_chip(term, k) for term, k in zip(sent, others)]
    all_blocks, pooled = lax.optimization_barrier((all_blocks, sent[-1]))
    all_docs = all_blocks[:, :, :width].reshape(all_count, width)
    low, middle, high = (
        all_blocks[:, :, at : at + pos_count].reshape(all_count, pos_count).astype(I32)
        for at in range(width, width + 3 * LANES, LANES)
    )
    all_positives = low + 256 * middle + 65536 * high

    info = lax.dynamic_slice_in_dim(all_blocks, lax.axis_index("grp") * shards, shards, 0)
    info = info[:, :, width + 3 * LANES :].astype(I32)
    owners = info[:, 0, :labels]
    rows = 256 * info[:, 0, labels:] + info[:, 1, :labels]
    marks = owners[:, None, :] == jnp.arange(shards, dtype=I32)[None, :, None]
    order = lax.broadcasted_iota(I32, (labels, labels), 0) < lax.broadcasted_iota(
        I32, (labels, labels), 1
    )
    before = jnp.dot(
        marks.reshape(shards * shards, labels).astype(BF16),
        order.astype(BF16),
        preferred_element_type=F32,
    ).reshape(shards, shards, labels)
    slot = jnp.sum(jnp.where(marks, before, 0.0), axis=1).astype(I32)
    slots = shards * label_cap
    source = jnp.arange(shards, dtype=I32)[:, None]
    coming = jnp.where(owners == me, (source ^ me) * label_cap + slot, -1).reshape(shards * labels)
    hit = jnp.arange(slots, dtype=I32)[:, None] == coming[None, :]
    got_rows = jnp.sum(jnp.where(hit, rows.reshape(shards * labels)[None, :] + 1, 0), axis=1) - 1
    going = jnp.where(
        (owners ^ me) % 2 == 0, ((owners ^ me) + (source ^ me) % 2) * label_cap + slot, -1
    )
    places = jnp.concatenate(
        [lax.dynamic_index_in_dim(going, me, 0, False), lax.dynamic_index_in_dim(going, me ^ 1, 0, False)]
    )
    to_slots = (jnp.arange(slots, dtype=I32)[:, None] == places[None, :]).astype(BF16)

    for term in arrived:
        pooled = pooled + term.astype(F32)
    pooled = pooled.astype(BF16)
    projected = jnp.dot(pooled, enc_weight, preferred_element_type=F32)
    norm_scale = lax.rsqrt(jnp.mean(projected * projected, axis=1, keepdims=True) + 1e-06)
    encoded = (projected * norm_scale * enc_gain * width ** (-0.5)).astype(BF16)

    both = jnp.concatenate([encoded, swap_cores(encoded)])
    send_vectors = jnp.dot(to_slots, both, preferred_element_type=F32).astype(BF16)
    send_vectors = send_vectors.reshape(chips, 2 * label_cap, width)
    arrived = {k: to_chip(send_vectors[k], k) for k in others}
    got_vectors = jnp.concatenate([send_vectors[0]] + [arrived[k] for k in range(1, chips)])
    to_rows = (jnp.arange(slab_rows, dtype=I32)[:, None] == got_rows[None, :]).astype(BF16)
    delta = jnp.dot(to_rows, got_vectors, preferred_element_type=F32)
    head = (free_rows.astype(F32) + delta).astype(BF16)

    label_columns = lax.axis_index(ALL) * slab_rows + jnp.arange(slab_rows, dtype=I32)
    logits = lax.dot_general(all_docs, head, (((1,), (1,)), ((), ())), preferred_element_type=F32)
    hits = jnp.zeros(logits.shape, jnp.bool_)
    for column in range(pos_count):
        hits = hits | (all_positives[:, column : column + 1] == label_columns[None, :])
    errors = (jax.nn.sigmoid(logits) - hits.astype(F32)).astype(BF16)
    doc_terms = jnp.dot(errors, head, preferred_element_type=F32)
    doc_terms = doc_terms.reshape(devices, own_docs, width)
    doc_terms, late_errors = lax.optimization_barrier((doc_terms, errors))
    doc_parts = exchange(doc_terms, ALL)
    picked = lax.dot_general(
        to_rows, late_errors, (((0,), (1,)), ((), ())), preferred_element_type=F32
    ).astype(BF16)
    picked = picked.reshape(chips, 2 * label_cap, all_count)
    arrived = {k: to_chip(picked[k], k) for k in others}
    returned = jnp.concatenate([picked[0]] + [arrived[k] for k in range(1, chips)])
    free_grad = rows_grad(errors, all_docs)
    returned, doc_parts, free_grad = lax.optimization_barrier((returned, doc_parts, free_grad))
    doc_grad = jnp.sum(doc_parts, axis=0)
    chip_errors = lax.dot_general(
        to_slots, returned, (((0,), (0,)), ((), ())), preferred_element_type=F32
    ).astype(BF16)
    ref_errors = chip_errors[:labels] + swap_cores(chip_errors[labels:])
    ref_grad = jnp.dot(ref_errors, all_docs, preferred_element_type=F32).astype(BF16)
    return (free_grad, doc_grad, ref_grad)


def on_device(token_table, enc_weight, enc_gain, label_tokens, *rest):
    shards = lax.axis_size("shard")
    labels, length = label_tokens.shape
    row_count = 5 * labels * length // 4
    plan = by_sums if shards % 2 == 0 and shards // 2 * labels < row_count else by_rows
    return plan(token_table, enc_weight, enc_gain, label_tokens, *rest)


def solution(mesh):
    in_specs = (
        P("shard", None),
        P(),
        P(),
        P(ALL, None),
        P(ALL, None),
        P(ALL),
        P(ALL, None),
        P(ALL, None),
        P(ALL, None),
    )
    out_specs = (P(ALL, None), P(ALL, None), P(ALL, None))
    return jax.shard_map(
        on_device, mesh=mesh, in_specs=in_specs, out_specs=out_specs, check_vma=False
    )
```

```python
import functools
import jax
import jax.numpy as jnp
from jax import lax
from jax.experimental import pallas as pl
from jax.experimental.pallas import tpu as pltpu
from jax.sharding import PartitionSpec as P

BF16 = jnp.bfloat16
F32 = jnp.float32
I32 = jnp.int32
ALL = ("grp", "shard")


def exchange(blocks, axes):
    return lax.all_to_all(blocks, axes, split_axis=0, concat_axis=0, tiled=True)


def inclusive_counts(marks):
    count = marks.shape[0]
    rows = lax.broadcasted_iota(I32, (count, count), 0)
    cols = lax.broadcasted_iota(I32, (count, count), 1)
    return jnp.dot((cols <= rows).astype(BF16), marks.astype(BF16), preferred_element_type=F32).astype(I32)


def token_places(owner, shards, cap):
    labels, length = owner.shape
    marks = (owner[:, :, None] == jnp.arange(shards, dtype=I32)).astype(I32)
    within = inclusive_counts(marks.reshape(labels, length * shards)).reshape(labels, length, shards)
    totals = within[-1]
    before = jnp.cumsum(totals, axis=0) - totals
    slot = jnp.sum((within + before[None] - 1) * marks, axis=2)
    return owner * cap + slot


def label_places(owner, shards, cap):
    marks = (owner[:, None] == jnp.arange(shards, dtype=I32)).astype(I32)
    slot = jnp.sum((inclusive_counts(marks) - 1) * marks, axis=1)
    return owner * cap + slot


def placed(values, places, size):
    hit = places[:, None] == jnp.arange(size, dtype=I32)[None, :]
    return jnp.sum(jnp.where(hit, values[:, None] + 1, 0), axis=0) - 1


def swap_cores(x):
    return lax.ppermute(x, "shard", [(i, i ^ 1) for i in range(lax.axis_size("shard"))])


def to_chip(x, k):
    return lax.ppermute(x, "shard", [(i, i ^ (2 * k)) for i in range(lax.axis_size("shard"))])


def by_rows(
    token_table, enc_weight, enc_gain, label_tokens, ref_owner, ref_row, free_rows, docs, positives
):
    shards = lax.axis_size("shard")
    devices = shards * lax.axis_size("grp")
    vocab_rows, width = token_table.shape
    labels, length = label_tokens.shape
    own_docs = docs.shape[0]
    pos_count = positives.shape[1]
    slab_rows = free_rows.shape[0]
    tokens = labels * length
    token_cap = 5 * tokens // (4 * shards)
    label_cap = 2 * labels // shards

    token_owner = label_tokens // vocab_rows
    token_dest = token_places(token_owner, shards, token_cap)
    send_ids = placed(
        (label_tokens - token_owner * vocab_rows).reshape(tokens),
        token_dest.reshape(tokens),
        shards * token_cap,
    )
    label_dest = label_places(ref_owner[:, 0], shards, label_cap)
    send_rows = placed(ref_row, label_dest, shards * label_cap)
    asked = exchange(
        jnp.concatenate(
            [send_ids.reshape(shards, token_cap), send_rows.reshape(shards, label_cap)], axis=1
        ),
        "shard",
    )
    got_rows = asked[:, token_cap:].reshape(shards * label_cap)

    digits = jnp.concatenate(
        [positives & 255, (positives >> 8) & 255, positives >> 16], axis=1
    ).astype(BF16)
    own_block = jnp.concatenate(
        [docs, digits, jnp.zeros((own_docs, 128 - 3 * pos_count), BF16)], axis=1
    )
    all_blocks = exchange(
        jnp.broadcast_to(own_block[None], (devices, own_docs, width + 128)), ALL
    ).reshape(devices * own_docs, width + 128)
    all_docs = all_blocks[:, :width]
    d = all_blocks[:, width : width + 3 * pos_count].astype(I32)
    all_positives = d[:, :pos_count] + 256 * d[:, pos_count : 2 * pos_count] + 65536 * d[:, 2 * pos_count :]

    found = token_table[jnp.maximum(asked[:, :token_cap], 0)]
    token_found = exchange(found, "shard").reshape(shards * token_cap, width)
    pick_tokens = jnp.zeros((labels, shards * token_cap), F32)
    for j in range(length):
        pick_tokens += (
            token_dest[:, j : j + 1] == jnp.arange(shards * token_cap, dtype=I32)[None, :]
        ).astype(F32)
    pooled = jnp.dot(
        (pick_tokens / length).astype(BF16), token_found, preferred_element_type=F32
    ).astype(BF16)
    projected = jnp.dot(pooled, enc_weight, preferred_element_type=F32)
    norm_scale = lax.rsqrt(jnp.mean(projected * projected, axis=1, keepdims=True) + 1e-06)
    encoded = (projected * norm_scale * enc_gain * width ** (-0.5)).astype(BF16)

    to_slots = (
        jnp.arange(shards * label_cap, dtype=I32)[:, None] == label_dest[None, :]
    ).astype(BF16)
    send_vectors = jnp.dot(to_slots, encoded, preferred_element_type=F32).astype(BF16)
    got_vectors = exchange(send_vectors.reshape(shards, label_cap, width), "shard").reshape(
        shards * label_cap, width
    )
    to_rows = (jnp.arange(slab_rows, dtype=I32)[:, None] == got_rows[None, :]).astype(BF16)
    delta = jnp.dot(to_rows, got_vectors, preferred_element_type=F32)
    head = (free_rows.astype(F32) + delta).astype(BF16)

    label_columns = lax.axis_index(ALL) * slab_rows + jnp.arange(slab_rows, dtype=I32)
    logits = lax.dot_general(all_docs, head, (((1,), (1,)), ((), ())), preferred_element_type=F32)
    hits = jnp.zeros(logits.shape, jnp.bool_)
    for column in range(pos_count):
        hits = hits | (all_positives[:, column : column + 1] == label_columns[None, :])
    errors = (jax.nn.sigmoid(logits) - hits.astype(F32)).astype(BF16)
    doc_terms = jnp.dot(errors, head, preferred_element_type=F32)
    free_grad = lax.dot_general(
        errors, all_docs, (((0,), (0,)), ((), ())), preferred_element_type=F32
    ).astype(BF16)
    picked = lax.dot_general(
        to_rows, errors, (((0,), (1,)), ((), ())), preferred_element_type=F32
    ).astype(BF16)
    returned = exchange(picked.reshape(shards, label_cap, devices * own_docs), "shard").reshape(
        shards * label_cap, devices * own_docs
    )
    ref_errors = lax.dot_general(
        to_slots, returned, (((0,), (0,)), ((), ())), preferred_element_type=F32
    ).astype(BF16)
    ref_grad = jnp.dot(ref_errors, all_docs, preferred_element_type=F32).astype(BF16)
    doc_grad = jnp.sum(exchange(doc_terms.reshape(devices, own_docs, width), ALL), axis=0)
    return (free_grad, doc_grad, ref_grad)


LANES = 128
SUBLANES = 8
PIECES = 12


def sum_kernel(count, moved, held, me_ref, *refs):
    ids_refs, (near_ref, far_ref), refs = refs[:count], refs[count : count + 2], refs[count + 2 :]
    refs = refs[1:] if held else refs
    sources, outs, targets = refs[:moved], refs[moved : moved + count], refs[moved + count : -7]
    note, stage, rows, sums, found, starts, sems = refs[-7:]
    note[...] = jnp.zeros(note.shape, F32)
    moves = [
        pltpu.make_async_copy(a, b, sems.at[2 * PIECES + 1 + n])
        for n, (a, b) in enumerate(zip(sources, targets))
    ]
    vocab_rows, width = near_ref.shape
    length, labels = ids_refs[0].shape
    chunks = width // LANES
    tile = SUBLANES * chunks
    piece = vocab_rows // PIECES
    core = me_ref[0] & 1
    bases = (core * vocab_rows, (1 - core) * vocab_rows)

    copies = []
    for half, table in enumerate((near_ref, far_ref)):
        for p in range(PIECES):
            at = half * PIECES + p
            copies.append(
                pltpu.make_async_copy(
                    table.at[pl.ds(p * piece, piece)],
                    stage.at[pl.ds(pl.multiple_of(bases[half] + p * piece, 16), piece)],
                    sems.at[at],
                )
            )
    for copy in copies + moves:
        copy.start()
    for n, ids_ref in enumerate(ids_refs):
        row = ids_ref[...] - (me_ref[0] >> 1) * (2 * vocab_rows)
        row = jnp.where((row >= 0) & (row < 2 * vocab_rows), row, 2 * vocab_rows)
        found[n * length : (n + 1) * length, :] = (row >> 3) * tile + (row & 7)
    place = pltpu.make_async_copy(found, starts, sems.at[2 * PIECES])
    place.start()
    rows[pl.ds(2 * vocab_rows * chunks, tile), :] = jnp.zeros((tile, LANES), F32)
    for at, copy in enumerate(copies):
        copy.wait()

        @pl.loop(0, piece // 16, unroll=5)
        def _(group):
            first = pl.multiple_of(bases[at // PIECES] + at % PIECES * piece + group * 16, 16)
            block = stage[pl.ds(first, 16), :].astype(F32)
            to = pl.multiple_of(first * chunks, 16)
            for h in range(2):
                for c in range(chunks):
                    rows[pl.ds(to + h * tile + c * SUBLANES, SUBLANES), :] = block[
                        h * SUBLANES : (h + 1) * SUBLANES, c * LANES : (c + 1) * LANES
                    ]

    place.wait()
    for n in range(count):

        @pl.loop(0, labels // SUBLANES, unroll=8)
        def _(group):
            for q in range(SUBLANES):
                label = group * SUBLANES + q
                terms = [
                    rows[pl.ds(starts[n * length + j, label], chunks, stride=SUBLANES), :]
                    for j in range(length)
                ]
                while len(terms) > 1:
                    terms = [a + b for a, b in zip(terms[::2], terms[1::2])] + terms[len(terms) // 2 * 2 :]
                to = (n * labels // SUBLANES + group) * tile + q
                sums[pl.ds(to, chunks, stride=SUBLANES), :] = terms[0] / length

    for copy in moves:
        copy.wait()
    for n, out in enumerate(outs):
        for group in range(labels // 16):
            for c in range(chunks):
                at = ((n * labels) // SUBLANES + 2 * group) * tile + c * SUBLANES
                out[16 * group : 16 * group + 16, c * LANES : (c + 1) * LANES] = jnp.concatenate(
                    [sums[at : at + SUBLANES, :], sums[at + tile : at + tile + SUBLANES, :]]
                ).astype(out.dtype)


def block_kernel(docs_ref, positives_ref, owner_ref, row_ref, out):
    count, width = docs_ref.shape
    devices, labels = out.shape[0], owner_ref.shape[1]
    positives, row = positives_ref[...], row_ref[...]

    def spread(value):
        return jnp.broadcast_to(value.astype(F32).astype(BF16)[None], (devices,) + value.shape)

    out[:, :, width:] = jnp.zeros((devices, count, out.shape[2] - width), BF16)
    out[:, :, :width] = jnp.broadcast_to(docs_ref[...][None], (devices, count, width))
    for n in range(3):
        at = width + n * LANES
        out[:, :, at : at + positives.shape[1]] = spread((positives >> (8 * n)) & 255)
    at = width + 3 * LANES
    second = jnp.concatenate([row & 255] + [jnp.zeros_like(row)] * (count - 1))
    first = jnp.concatenate([owner_ref[...], second[:-1]])
    out[:, :, at : at + labels] = spread(first)
    out[:, :, at + labels : at + 2 * labels] = spread(
        jnp.concatenate([row >> 8] + [jnp.zeros_like(row)] * (count - 1))
    )


def docs_block(docs, positives, ref_owner, ref_row, devices):
    count, width = docs.shape
    labels = ref_row.shape[0]
    return pl.pallas_call(
        block_kernel,
        out_shape=jax.ShapeDtypeStruct((devices, count, width + 3 * LANES + 2 * labels), BF16),
        in_specs=[pl.BlockSpec(memory_space=pltpu.VMEM)] * 4,
        out_specs=pl.BlockSpec(memory_space=pltpu.VMEM),
    )(docs, positives, ref_owner.reshape(1, labels), ref_row.reshape(1, labels))


def partial_means(me, ids, near, far, after, kinds, later=()):
    vocab_rows, width = near.shape
    chunks = width // LANES
    length, labels = ids[0].shape
    held = [] if after is None else [after]
    return pl.pallas_call(
        functools.partial(sum_kernel, len(kinds), len(later), bool(held)),
        out_shape=[jax.ShapeDtypeStruct((labels, width), kind) for kind in kinds]
        + [jax.ShapeDtypeStruct(x.shape, x.dtype) for x in later]
        + [jax.ShapeDtypeStruct((SUBLANES, LANES), F32)],
        in_specs=[pl.BlockSpec(memory_space=pltpu.SMEM)]
        + [pl.BlockSpec(memory_space=pltpu.VMEM)] * len(ids)
        + [pl.BlockSpec(memory_space=pl.ANY)] * 2
        + [pl.BlockSpec(memory_space=pltpu.VMEM) for _ in held]
        + [pl.BlockSpec(memory_space=pl.ANY) for _ in later],
        out_specs=[pl.BlockSpec(memory_space=pltpu.VMEM)] * (len(kinds) + len(later) + 1),
        scratch_shapes=[
            pltpu.VMEM((2 * vocab_rows, width), BF16),
            pltpu.VMEM(((2 * vocab_rows + 2 * SUBLANES) * chunks, LANES), F32),
            pltpu.VMEM(((len(kinds) * labels + SUBLANES) * chunks, LANES), F32),
            pltpu.VMEM((len(ids) * length, labels), I32),
            pltpu.SMEM((len(ids) * length, labels), I32),
            pltpu.SemaphoreType.DMA((2 * PIECES + 1 + len(later),)),
        ],
        compiler_params=pltpu.CompilerParams(
            vmem_limit_bytes=(56 if after is None else 52) * 1024 * 1024
        ),
        cost_estimate=pl.CostEstimate(
            flops=len(kinds) * labels * length * width,
            bytes_accessed=4 * vocab_rows * width,
            transcendentals=0,
        ),
    )(me, *ids, near, far, *held, *later)


def terms_kernel(errors_ref, head_ref, out_ref):
    terms = jnp.dot(errors_ref[...], head_ref[...], preferred_element_type=F32)
    devices, own_docs, _ = out_ref.shape
    for d in range(devices):
        out_ref[d, :, :] = terms[d * own_docs : (d + 1) * own_docs, :]


def terms_by_device(errors, head, devices):
    return pl.pallas_call(
        terms_kernel,
        out_shape=jax.ShapeDtypeStruct((devices, errors.shape[0] // devices, head.shape[1]), F32),
        in_specs=[pl.BlockSpec(memory_space=pltpu.VMEM)] * 2,
        out_specs=pl.BlockSpec(memory_space=pltpu.VMEM),
        compiler_params=pltpu.CompilerParams(vmem_limit_bytes=16 * 1024 * 1024),
    )(errors, head)


def grad_kernel(errors_ref, docs_ref, out_ref):
    out_ref[...] = lax.dot_general(
        errors_ref[...], docs_ref[...], (((0,), (0,)), ((), ())), preferred_element_type=F32
    ).astype(BF16)


def rows_grad(errors, docs):
    count, slab_rows = errors.shape
    width = docs.shape[1]
    step = 256 if slab_rows % 256 == 0 else slab_rows
    return pl.pallas_call(
        grad_kernel,
        grid=(slab_rows // step,),
        out_shape=jax.ShapeDtypeStruct((slab_rows, width), BF16),
        in_specs=[
            pl.BlockSpec((count, step), lambda i: (0, i)),
            pl.BlockSpec((count, width), lambda i: (0, 0)),
        ],
        out_specs=pl.BlockSpec((step, width), lambda i: (i, 0)),
        compiler_params=pltpu.CompilerParams(vmem_limit_bytes=16 * 1024 * 1024),
        cost_estimate=pl.CostEstimate(flops=1, bytes_accessed=1, transcendentals=0),
    )(errors, docs)


def by_sums(
    token_table, enc_weight, enc_gain, label_tokens, ref_owner, ref_row, free_rows, docs, positives
):
    shards = lax.axis_size("shard")
    chips = shards // 2
    devices = shards * lax.axis_size("grp")
    me = lax.axis_index("shard")
    vocab_rows, width = token_table.shape
    labels, length = label_tokens.shape
    own_docs = docs.shape[0]
    all_count = devices * own_docs
    pos_count = positives.shape[1]
    slab_rows = free_rows.shape[0]
    tokens = labels * length
    label_cap = 2 * labels // shards
    others = [k for k in range(chips - 1, 0, -1)]

    other_table = swap_cores(token_table)

    ids = label_tokens.T
    asked = {k: to_chip(ids, k) for k in others}
    asked[0] = ids

    own_blocks = docs_block(docs, positives, ref_owner, ref_row, devices)
    own_blocks, asked = lax.optimization_barrier((own_blocks, asked))
    all_blocks = exchange(own_blocks, ALL)

    sent, after = [], None
    half = len(others) - len(others) // 3
    for ks in (others[:half], others[half:] + [0]):
        later = () if after is None else (free_rows, enc_weight)
        *terms, note = partial_means(
            me.reshape(1), [asked[k] for k in ks], token_table, other_table, after,
            [BF16 if k else F32 for k in ks], later
        )
        if later:
            *terms, free_rows, enc_weight = terms
        sent += terms
        after = swap_cores(note)
    arrived = [to_chip(term, k) for term, k in zip(sent, others)]
    all_blocks, pooled = lax.optimization_barrier((all_blocks, sent[-1]))
    all_docs = all_blocks[:, :, :width].reshape(all_count, width)
    low, middle, high = (
        all_blocks[:, :, at : at + pos_count].reshape(all_count, pos_count).astype(I32)
        for at in range(width, width + 3 * LANES, LANES)
    )
    all_positives = low + 256 * middle + 65536 * high

    info = lax.dynamic_slice_in_dim(all_blocks, lax.axis_index("grp") * shards, shards, 0)
    info = info[:, :, width + 3 * LANES :].astype(I32)
    owners = info[:, 0, :labels]
    rows = 256 * info[:, 0, labels:] + info[:, 1, :labels]
    marks = owners[:, None, :] == jnp.arange(shards, dtype=I32)[None, :, None]
    order = lax.broadcasted_iota(I32, (labels, labels), 0) < lax.broadcasted_iota(
        I32, (labels, labels), 1
    )
    before = jnp.dot(
        marks.reshape(shards * shards, labels).astype(BF16),
        order.astype(BF16),
        preferred_element_type=F32,
    ).reshape(shards, shards, labels)
    slot = jnp.sum(jnp.where(marks, before, 0.0), axis=1).astype(I32)
    slots = shards * label_cap
    source = jnp.arange(shards, dtype=I32)[:, None]
    coming = jnp.where(owners == me, (source ^ me) * label_cap + slot, -1).reshape(shards * labels)
    hit = jnp.arange(slots, dtype=I32)[:, None] == coming[None, :]
    got_rows = jnp.sum(jnp.where(hit, rows.reshape(shards * labels)[None, :] + 1, 0), axis=1) - 1
    going = jnp.where(
        (owners ^ me) % 2 == 0, ((owners ^ me) + (source ^ me) % 2) * label_cap + slot, -1
    )
    places = jnp.concatenate(
        [lax.dynamic_index_in_dim(going, me, 0, False), lax.dynamic_index_in_dim(going, me ^ 1, 0, False)]
    )
    to_slots = (jnp.arange(slots, dtype=I32)[:, None] == places[None, :]).astype(BF16)

    for term in arrived:
        pooled = pooled + term.astype(F32)
    pooled = pooled.astype(BF16)
    projected = jnp.dot(pooled, enc_weight, preferred_element_type=F32)
    norm_scale = lax.rsqrt(jnp.mean(projected * projected, axis=1, keepdims=True) + 1e-06)
    encoded = (projected * norm_scale * enc_gain * width ** (-0.5)).astype(BF16)

    both = jnp.concatenate([encoded, swap_cores(encoded)])
    send_vectors = jnp.dot(to_slots, both, preferred_element_type=F32).astype(BF16)
    send_vectors = send_vectors.reshape(chips, 2 * label_cap, width)
    arrived = {k: to_chip(send_vectors[k], k) for k in others}
    got_vectors = jnp.concatenate([send_vectors[0]] + [arrived[k] for k in range(1, chips)])
    to_rows = (jnp.arange(slab_rows, dtype=I32)[:, None] == got_rows[None, :]).astype(BF16)
    delta = jnp.dot(to_rows, got_vectors, preferred_element_type=F32)
    head = (free_rows.astype(F32) + delta).astype(BF16)

    label_columns = lax.axis_index(ALL) * slab_rows + jnp.arange(slab_rows, dtype=I32)
    logits = lax.dot_general(all_docs, head, (((1,), (1,)), ((), ())), preferred_element_type=F32)
    hits = jnp.zeros(logits.shape, jnp.bool_)
    for column in range(pos_count):
        hits = hits | (all_positives[:, column : column + 1] == label_columns[None, :])
    errors = (jax.nn.sigmoid(logits) - hits.astype(F32)).astype(BF16)
    doc_terms = terms_by_device(errors, head, devices)
    doc_terms, late_errors = lax.optimization_barrier((doc_terms, errors))
    doc_parts = exchange(doc_terms, ALL)
    picked = lax.dot_general(
        to_rows, late_errors, (((0,), (1,)), ((), ())), preferred_element_type=F32
    ).astype(BF16)
    picked = picked.reshape(chips, 2 * label_cap, all_count)
    arrived = {k: to_chip(picked[k], k) for k in others}
    returned = jnp.concatenate([picked[0]] + [arrived[k] for k in range(1, chips)])
    free_grad = rows_grad(errors, all_docs)
    returned, doc_parts, free_grad = lax.optimization_barrier((returned, doc_parts, free_grad))
    doc_grad = jnp.sum(doc_parts, axis=0)
    chip_errors = lax.dot_general(
        to_slots, returned, (((0,), (0,)), ((), ())), preferred_element_type=F32
    ).astype(BF16)
    ref_errors = chip_errors[:labels] + swap_cores(chip_errors[labels:])
    ref_grad = jnp.dot(ref_errors, all_docs, preferred_element_type=F32).astype(BF16)
    return (free_grad, doc_grad, ref_grad)


def on_device(token_table, enc_weight, enc_gain, label_tokens, *rest):
    shards = lax.axis_size("shard")
    labels, length = label_tokens.shape
    row_count = 5 * labels * length // 4
    plan = by_sums if shards % 2 == 0 and shards // 2 * labels < row_count else by_rows
    return plan(token_table, enc_weight, enc_gain, label_tokens, *rest)


def solution(mesh):
    in_specs = (
        P("shard", None),
        P(),
        P(),
        P(ALL, None),
        P(ALL, None),
        P(ALL),
        P(ALL, None),
        P(ALL, None),
        P(ALL, None),
    )
    out_specs = (P(ALL, None), P(ALL, None), P(ALL, None))
    return jax.shard_map(
        on_device, mesh=mesh, in_specs=in_specs, out_specs=out_specs, check_vma=False
    )
```
